128 devices in a mesh: gx: 4 (over y), gy: 32 (over x, z, core).
Axes of the slice: x: 4, y: 4, z: 4, core: 2. Of those that a mesh axis runs over, the one named last changes fastest.
Arguments:
- parents: bfloat16 [1024, 64, 256], P(('gx', 'gy')), may hold values from -6 to 6
- parent_dest: int32 [1024], P(('gx', 'gy')), may hold values from -1 to 511, as said below
- skip: bfloat16 [1024, 512, 128], P(('gx', 'gy')), may hold values from -6 to 6
- skip_dest: int32 [1024], P(('gx', 'gy')), may hold values from -1 to 511, as said below
- neighbours: int32 [512, 26], P(('gx', 'gy')), may hold values from -1 to 511, as said below
- up_weight: bfloat16 [8, 256, 128], replicated, may hold values from -0.375 to 0.375
- conv_weight: bfloat16 [27, 256, 128], replicated, may hold values from -0.078125 to 0.078125
Outputs:
- refined: bfloat16 [512, 512, 128], P(('gx', 'gy'))
The draws below stay inside these ranges and needn't reach their ends.
Inputs may be any that keep to these rules, and one draw needn't show every extreme that they name: `parent_dest`: each child brick index appears exactly once. Child brick c belongs to device c // 4 of the flattened axis gx+gy (gx slowest) and to its slot c % 4; it lies on a device with the same gx index as the slot that names it. One device names at most 1 child bricks of any one device, and in every draw some device names exactly 1 of one device. In every draw some device has all 8 of its slots live. `skip_dest`: each child brick index appears exactly once. Child brick c belongs to device c // 4 of the flattened axis gx+gy (gx slowest) and to its slot c % 4; it lies on a device with the same gx index as the slot that names it. One device names at most 1 child bricks of any one device, and in every draw some device names exactly 1 of one device. In every draw some device has all 8 of its slots live. Direction k = 0..25 enumerates (dx, dy, dz) in the finite set (-1,0,1)^3 with dx slowest and dz fastest, (0,0,0) left out. neighbours[c, k] is the child brick displaced from brick c by (dx, dy, dz) in the brick lattice, or -1 where no brick is there; the relation is symmetric. A brick's neighbours belong to its own device or to the devices just before and just after it on the flattened axis gx+gy.
All inputs are finite; a program needn't handle non-finite values.
Results may differ from the reference program's by a relative error of at most 0.0039.
Values may be sent and summed in bfloat16 or wider, within the bound.
No kernel may reach another device: no remote copies, remote signals or barrier semaphores. Data moves between devices by JAX's collectives and lax.ppermute only.
A program may use at most 64 MiB of HBM per device.

```python
import jax
import jax.numpy as jnp
import numpy as np
from jax import lax

C_PARENT = 256
C_CHILD = 128
C_SKIP = 128
C_OUT = 128
BRICKS_DEV = 4
SLOTS_DEV = 8
SLOTS = 1024
N_GX = 4
N_GY = 32


neighbour_steps = [(code // 9 - 1, code // 3 % 3 - 1, code % 3 - 1) for code in range(27) if code != 13]


def owner_lists(key):
    bricks_dev = BRICKS_DEV
    slot_count = SLOTS_DEV
    gy_count = N_GY
    subkeys = jax.random.split(key, 4)
    row_keys = jax.random.split(subkeys[0], N_GX)

    def row_counts(row_key):
        perm_key, move_key = jax.random.split(row_key)
        shuffled = jax.random.permutation(perm_key, gy_count)
        transfers = jax.random.randint(move_key, (gy_count,), 0, bricks_dev)
        position = jnp.arange(gy_count)
        pair_idx = jnp.maximum(position - 3, 0) // 2
        is_first = (position >= 3) & ((position - 3) % 2 == 0)
        has_partner = position + 1 < gy_count
        amount = transfers[pair_idx]
        by_pos = jnp.where(is_first, jnp.where(has_partner, bricks_dev + amount, bricks_dev), bricks_dev - amount)
        by_pos = jnp.where(position == 0, slot_count, by_pos)
        by_pos = jnp.where(position == 1, 1, by_pos)
        by_pos = jnp.where(position == 2, bricks_dev - 1, by_pos)
        return jnp.zeros((gy_count,), jnp.int32).at[shuffled].set(by_pos.astype(jnp.int32))
    counts = jax.vmap(row_counts)(row_keys)
    starts = jnp.cumsum(counts, axis=1) - counts
    rotation = jax.random.randint(subkeys[1], (N_GX, 1, 1), 0, gy_count)
    dev_keys = jax.random.split(subkeys[2], N_GX * gy_count)

    def slot_ranking(dev_key):
        return jax.random.permutation(dev_key, slot_count)
    ranking = jax.vmap(slot_ranking)(dev_keys).reshape(N_GX, gy_count, slot_count)
    order_index = starts[:, :, None] + ranking
    owners = (order_index + rotation) % gy_count
    landing = order_index // gy_count
    row_index = jnp.arange(N_GX)[:, None, None]
    child_id = (row_index * gy_count + owners) * bricks_dev + landing
    return jnp.where(ranking < counts[:, :, None], child_id, -1).reshape(-1).astype(jnp.int32)


def draw_parent_dest(key, part):
    return owner_lists(jax.random.fold_in(key, 11))


def draw_skip_dest(key, part):
    return owner_lists(jax.random.fold_in(key, 23))


def draw_neighbours(key, part):
    owner_count = N_GX * N_GY
    bricks_dev = BRICKS_DEV
    layers = bricks_dev // 2
    depth = owner_count * layers
    dev_keys = jax.random.split(jax.random.fold_in(key, 37), owner_count)

    def cell_choice(dev_key):
        return jax.random.permutation(dev_key, 2 * bricks_dev)[:bricks_dev]
    cells = jax.vmap(cell_choice)(dev_keys)
    cell_x = (cells % 2).reshape(-1)
    cell_y = (cells // 2 % 2).reshape(-1)
    cell_z = (cells // 4 + jnp.arange(owner_count)[:, None] * layers).reshape(-1)
    brick_ids = jnp.arange(owner_count * bricks_dev, dtype=jnp.int32)
    lattice = jnp.full((4 * depth,), -1, jnp.int32).at[(cell_x * 2 + cell_y) * depth + cell_z].set(brick_ids)
    steps_table = jnp.asarray(np.array(neighbour_steps, dtype=np.int32))
    near_x = cell_x[:, None] + steps_table[None, :, 0]
    near_y = cell_y[:, None] + steps_table[None, :, 1]
    near_z = cell_z[:, None] + steps_table[None, :, 2]
    inside = (near_x >= 0) & (near_x < 2) & (near_y >= 0) & (near_y < 2) & (near_z >= 0) & (near_z < depth)
    flat_cell = (jnp.clip(near_x, 0, 1) * 2 + jnp.clip(near_y, 0, 1)) * depth + jnp.clip(near_z, 0, depth - 1)
    return jnp.where(inside, lattice[flat_cell], -1).astype(jnp.int32)


def level_of(rng, shape, cuts, low, largest):
    gain, own = 1.0, jax.random.fold_in(rng, 6)
    for dim, shards_of in cuts:
        steps = jnp.exp(jax.random.uniform(jax.random.fold_in(own, dim), (shards_of,), jnp.float32, low / len(cuts), largest / len(cuts)))
        gain = gain * jnp.repeat(steps, shape[dim] // shards_of).reshape([-1 if axis == dim else 1 for axis in range(len(shape))])
    return gain


def normal_values(own_key, extent, spread, reach, cuts=(), held_as=jnp.bfloat16):
    values = spread * jax.random.normal(own_key, extent, jnp.float32)
    if cuts:
        values = values * level_of(own_key, extent, cuts, -0.22, 0.18)
    return jnp.clip(values, -reach, reach).astype(held_as)


def setup_inputs(seed: int = 0) -> dict:
    arg_keys = jax.random.split(jax.random.key(seed), 8)
    return {
        "parents": normal_values(arg_keys[0], (SLOTS, 64, C_PARENT), 1.0, 6.0, ((0, 128),)),
        "parent_dest": draw_parent_dest(jax.random.fold_in(arg_keys[7], 71), 0),
        "skip": normal_values(arg_keys[2], (SLOTS, 512, C_SKIP), 1.0, 6.0, ((0, 128),)),
        "skip_dest": draw_skip_dest(jax.random.fold_in(arg_keys[7], 71), 0),
        "neighbours": draw_neighbours(jax.random.fold_in(arg_keys[7], 71), 0),
        "up_weight": normal_values(arg_keys[5], (8, C_PARENT, C_CHILD), C_PARENT ** -0.5, 0.375),
        "conv_weight": normal_values(arg_keys[6], (27, C_CHILD + C_SKIP, C_OUT), (27 * (C_CHILD + C_SKIP)) ** -0.5, 0.078125),
    }


neighbour_steps = [(code // 9 - 1, (code // 3) % 3 - 1, code % 3 - 1) for code in range(27) if code != 13]


def edge_range(offset):
    if offset < 0:
        return slice(7, 8)
    if offset > 0:
        return slice(0, 1)
    return slice(0, 8)


def upsample(bricks_in, up_weight):
    brick_count = bricks_in.shape[0]
    product = jnp.einsum("nvc,tcd->nvtd", bricks_in.astype(jnp.float32), up_weight.astype(jnp.float32))
    product = product.reshape(brick_count, 4, 4, 4, 2, 2, 2, up_weight.shape[2])
    product = product.transpose(0, 1, 4, 2, 5, 3, 6, 7)
    return product.reshape(brick_count, 512, up_weight.shape[2]).astype(jnp.bfloat16)


def faces_of(volume):
    return jnp.stack([volume[:, 0], volume[:, 7], volume[:, :, 0], volume[:, :, 7], volume[:, :, :, 0], volume[:, :, :, 7]], axis=1)


def assemble(center, faces_pool, lookup):
    pieces = {}
    for direction, (off_x, off_y, off_z) in enumerate(neighbour_steps):
        if off_x != 0:
            surface = faces_pool[:, 1 if off_x < 0 else 0][:, edge_range(off_y), edge_range(off_z)][:, None]
        elif off_y != 0:
            surface = faces_pool[:, 3 if off_y < 0 else 2][:, edge_range(off_x), edge_range(off_z)][:, :, None]
        else:
            surface = faces_pool[:, 5 if off_z < 0 else 4][:, edge_range(off_x), edge_range(off_y)][:, :, :, None]
        column = lookup[:, direction]
        picked = jnp.take(surface, jnp.maximum(column, 0), axis=0)
        pieces[(off_x, off_y, off_z)] = jnp.where((column >= 0)[:, None, None, None, None], picked, jnp.zeros((), picked.dtype))
    pieces[(0, 0, 0)] = center
    return jnp.concatenate([jnp.concatenate([jnp.concatenate([pieces[(off_x, off_y, off_z)] for off_z in (-1, 0, 1)], axis=3) for off_y in (-1, 0, 1)], axis=2) for off_x in (-1, 0, 1)], axis=1)


def convolve(padded, conv_weight):
    brick_count = padded.shape[0]
    rows_all = brick_count * 512
    result = jnp.zeros((rows_all, conv_weight.shape[2]), jnp.float32)
    for tap_index in range(27):
        start_x, start_y, start_z = tap_index // 9, (tap_index // 3) % 3, tap_index % 3
        window = padded[:, start_x:start_x + 8, start_y:start_y + 8, start_z:start_z + 8, :].reshape(rows_all, padded.shape[-1])
        result = result + jnp.dot(window, conv_weight[tap_index], preferred_element_type=jnp.float32)
    return jnp.maximum(result, 0.0).astype(jnp.bfloat16).reshape(brick_count, 512, conv_weight.shape[2])


def reference(parents, parent_dest, skip, skip_dest, neighbours, up_weight, conv_weight):
    brick_total = neighbours.shape[0]
    slot_ids = jnp.arange(parent_dest.shape[0], dtype=jnp.int32)
    parent_of = jnp.zeros((brick_total,), jnp.int32).at[jnp.where(parent_dest >= 0, parent_dest, brick_total)].set(slot_ids, mode="drop")
    skip_of = jnp.zeros((brick_total,), jnp.int32).at[jnp.where(skip_dest >= 0, skip_dest, brick_total)].set(slot_ids, mode="drop")
    block_size = 64
    group_count = brick_total // block_size

    def build_group(group_index):
        first = (group_index * block_size).astype(jnp.int32)
        chosen = lax.dynamic_slice_in_dim(parent_of, first, block_size)
        child_block = upsample(jnp.take(parents, chosen, axis=0), up_weight)
        skip_block = jnp.take(skip, lax.dynamic_slice_in_dim(skip_of, first, block_size), axis=0)
        return jnp.concatenate([child_block, skip_block], axis=-1)

    features = lax.map(build_group, jnp.arange(group_count, dtype=jnp.int32))
    features = features.reshape(brick_total, 8, 8, 8, features.shape[-1])
    faces_pool = faces_of(features)

    def refine(inputs):
        center, lookup = inputs
        return convolve(assemble(center, faces_pool, lookup), conv_weight)

    refined = lax.map(refine, (features.reshape(group_count, block_size, 8, 8, 8, features.shape[-1]), neighbours.reshape(group_count, block_size, 26)))
    return refined.reshape(brick_total, 512, conv_weight.shape[2])
```

```python
import jax
import jax.numpy as jnp
from jax import lax
from jax.experimental import pallas as pl
from jax.experimental.pallas import tpu as pltpu
from jax.sharding import PartitionSpec as P

LINES, COLUMNS = 4, 8
SLOTS, BRICKS = 8, 4
SKIP_ROWS, PARENT_ROWS, HEAD_ROWS = 512, 128, 16
BODY = SKIP_ROWS + PARENT_ROWS
DEPTH = 2
PIECES = ((SKIP_ROWS, 0, 0), (PARENT_ROWS, SKIP_ROWS, SKIP_ROWS * DEPTH))
BF16, F32, I32 = jnp.bfloat16, jnp.float32, jnp.int32

ANY = pl.BlockSpec(memory_space=pl.ANY)
SMEM = pl.BlockSpec(memory_space=pltpu.SMEM)
VMEM = pl.BlockSpec(memory_space=pltpu.VMEM)


def rows_of(shape, values):
    row = lax.broadcasted_iota(I32, shape, 0)
    out = jnp.full(shape, -1, I32)
    for j, value in enumerate(values):
        out = jnp.where(row == j, value, out)
    return out


def first_kernel(parent_dest, skip_dest, base, parents, skip, out, slot_of, sems):
    for q in range(2 * COLUMNS + 1):
        slot_of[q] = 0
    table = []
    for kind, dest in enumerate((skip_dest, parent_dest)):
        for s in range(SLOTS):
            d = dest[s]
            local = jnp.where(d >= 0, d - base[0], -1)
            table.append(local)
            column = lax.rem(lax.div(jnp.maximum(local, 0), BRICKS), COLUMNS)
            slot_of[jnp.where(d >= 0, kind * COLUMNS + column, 2 * COLUMNS)] = s
    copies = []
    for q in range(COLUMNS):
        s, p = slot_of[q], slot_of[COLUMNS + q]
        copies.append(pltpu.make_async_copy(skip.at[s], out.at[q, 0:512], sems.at[q, 0]))
        for half in range(2):
            copies.append(
                pltpu.make_async_copy(
                    parents.at[p, :, 128 * half : 128 * half + 128],
                    out.at[q, 512 + 64 * half : 576 + 64 * half],
                    sems.at[q, 1 + half],
                )
            )
    for copy in copies:
        copy.start()
    header = rows_of((HEAD_ROWS, 128), table).astype(F32).astype(BF16)
    for q in range(COLUMNS):
        out[q, BODY : BODY + HEAD_ROWS] = header
    for copy in copies:
        copy.wait()


def first_pack(parent_dest, skip_dest, base, parents, skip):
    return pl.pallas_call(
        first_kernel,
        out_shape=jax.ShapeDtypeStruct((COLUMNS, BODY + HEAD_ROWS, 128), BF16),
        in_specs=[SMEM, SMEM, SMEM, ANY, ANY],
        out_specs=VMEM,
        scratch_shapes=[
            pltpu.SMEM((2 * COLUMNS + 1,), I32),
            pltpu.SemaphoreType.DMA((COLUMNS, 3)),
        ],
        compiler_params=pltpu.CompilerParams(vmem_limit_bytes=16 * 2**20),
    )(parent_dest, skip_dest, base, parents, skip)


def second_kernel(place, came, *refs):
    outs = refs[:LINES]
    found, table, counts, source, landing, sem = refs[LINES:]
    line, column = place[0], place[1]
    for j in range(2 * LINES + 1):
        counts[j] = 0
    for j in range(2 * LINES * DEPTH + 1):
        source[j] = 0
        landing[j] = -1
    lane = lax.broadcasted_iota(I32, (COLUMNS, SLOTS, 128), 2)
    over = jnp.zeros((1, 128), I32)
    picks = []
    every = came[:, BODY : BODY + HEAD_ROWS].astype(F32).astype(I32)
    for kind in range(2):
        dest = every[:, kind * SLOTS : kind * SLOTS + SLOTS]
        live = dest >= 0
        owner = dest >> 2
        its_column = owner & 7
        mine = jnp.where(live & (its_column == column), dest, -1)
        picks.append(jnp.max(mine, axis=1))
        to_column = jnp.where(live & (its_column == lane), 1, 0)
        over = over | jnp.where(
            jnp.max(jnp.sum(to_column, axis=1), axis=0, keepdims=True) > 1, 1, 0
        )
        to_owner = jnp.where(live & (owner == lane), 1, 0)
        total = jnp.sum(jnp.sum(to_owner, axis=1), axis=0, keepdims=True)
        over = over | jnp.where(total > DEPTH, 1, 0)
    flag = jnp.max(over.astype(F32), axis=1, keepdims=True).astype(I32)
    lane = lax.broadcasted_iota(I32, (COLUMNS, 128), 1)
    found[...] = jnp.where(lane == 0, picks[0], picks[1])
    copy = pltpu.make_async_copy(found, table, sem)
    copy.start()
    copy.wait()
    for kind in range(2):
        for m in range(COLUMNS):
            dest = table[m, kind]
            live = dest >= 0
            to_line = jnp.where(live, dest >> 5, 0)
            count_at = jnp.where(live, kind * LINES + to_line, 2 * LINES)
            rank = counts[count_at]
            counts[count_at] = rank + 1
            spot = jnp.where(
                live & (rank < DEPTH),
                (kind * LINES + to_line) * DEPTH + rank,
                2 * LINES * DEPTH,
            )
            source[spot] = m
            landing[spot] = dest & 3
    for k in range(LINES):
        to_line = lax.rem(line + k, LINES)
        spots = []
        for kind, (rows, first, height) in enumerate(PIECES):
            for r in range(DEPTH):
                spot = (kind * LINES + to_line) * DEPTH + r
                spots.append(landing[spot])
                outs[k][height + r * rows : height + r * rows + rows] = came[
                    source[spot], first : first + rows
                ]
        outs[k][BODY * DEPTH : BODY * DEPTH + HEAD_ROWS] = (
            rows_of((HEAD_ROWS, 128), spots + [flag]).astype(F32).astype(BF16)
        )


def second_pack(place, came):
    message = jax.ShapeDtypeStruct((BODY * DEPTH + HEAD_ROWS, 128), BF16)
    return pl.pallas_call(
        second_kernel,
        out_shape=[message] * LINES,
        in_specs=[SMEM, VMEM],
        out_specs=[VMEM] * LINES,
        scratch_shapes=[
            pltpu.VMEM((COLUMNS, 128), I32),
            pltpu.SMEM((COLUMNS, 128), I32),
            pltpu.SMEM((2 * LINES + 1,), I32),
            pltpu.SMEM((2 * LINES * DEPTH + 1,), I32),
            pltpu.SMEM((2 * LINES * DEPTH + 1,), I32),
            pltpu.SemaphoreType.DMA,
        ],
        compiler_params=pltpu.CompilerParams(vmem_limit_bytes=16 * 2**20),
    )(place, came)


def unpack_kernel(*refs):
    came = refs[:LINES]
    own, flag_out, found, table, sem = refs[LINES:]
    lane = lax.broadcasted_iota(I32, (HEAD_ROWS, 128), 1)
    row = lax.broadcasted_iota(I32, (HEAD_ROWS, 128), 0)
    for k in range(LINES):
        header = came[k][BODY * DEPTH : BODY * DEPTH + HEAD_ROWS].astype(F32)
        found[k : k + 1] = jnp.sum(
            jnp.where(lane == row, header, 0.0), axis=0, keepdims=True
        ).astype(I32)
    found[LINES:8] = jnp.zeros((8 - LINES, 128), I32)
    copy = pltpu.make_async_copy(found, table, sem)
    copy.start()
    copy.wait()
    flag = table[0, 2 * DEPTH]
    for k in range(1, LINES):
        flag = flag | table[k, 2 * DEPTH]
    flag_out[0] = flag
    for k in range(LINES):
        for kind, (rows, first, height) in enumerate(PIECES):
            for r in range(DEPTH):
                brick = table[k, kind * DEPTH + r]

                @pl.when(brick >= 0)
                def _(k=k, rows=rows, first=first, at=height + r * rows, brick=brick):
                    own[brick, first : first + rows] = came[k][at : at + rows]


def unpack(messages):
    return pl.pallas_call(
        unpack_kernel,
        out_shape=[
            jax.ShapeDtypeStruct((BRICKS, BODY, 128), BF16),
            jax.ShapeDtypeStruct((1,), I32),
        ],
        in_specs=[VMEM] * LINES,
        out_specs=[VMEM, SMEM],
        scratch_shapes=[
            pltpu.VMEM((8, 128), I32),
            pltpu.SMEM((8, 128), I32),
            pltpu.SemaphoreType.DMA,
        ],
        compiler_params=pltpu.CompilerParams(vmem_limit_bytes=16 * 2**20),
    )(*messages)


def dense_route(parents, parent_dest, skip, skip_dest):
    halves = parents.reshape(SLOTS, 64, 2, 128).transpose(0, 2, 1, 3).reshape(SLOTS, 128, 128)
    joined = []
    for dest, payload in ((skip_dest, skip), (parent_dest, halves)):
        devices = LINES * COLUMNS
        owner = jnp.where(dest >= 0, dest // BRICKS % devices, -1)
        match = owner[None, :] == jnp.arange(devices)[:, None]
        spot = jnp.sum(jnp.where(match, dest % BRICKS + 1, 0), axis=1) - 1
        rows = jnp.einsum(
            "os,src->orc", match.astype(BF16), payload, preferred_element_type=F32
        ).astype(BF16)
        rows = lax.all_to_all(rows, "gy", 0, 0, tiled=True)
        spot = lax.all_to_all(spot, "gy", 0, 0, tiled=True)
        pick = spot[None, :] == jnp.arange(BRICKS)[:, None]
        joined.append(
            jnp.einsum(
                "bo,orc->brc", pick.astype(BF16), rows, preferred_element_type=F32
            ).astype(BF16)
        )
    return jnp.concatenate(joined, axis=1)


def conv_kernel(
    lookup, before, own, after, up_weight, conv_weight, out, pool, shifted, window
):
    row = lax.broadcasted_iota(I32, (256, 64), 0)
    column = lax.broadcasted_iota(I32, (256, 64), 1)
    in_brick = row & 127
    takes = (in_brick >> 3) * 4 + ((in_brick & 7) >> 1) == column
    spread = jnp.where(takes & ((row & 1) == (row >> 7)), 1.0, 0.0).astype(BF16)
    for group, bricks in enumerate((before, own, after)):
        spaced = []
        for b in range(BRICKS):
            pool[group * BRICKS + b, :, :, :, 128:256] = (
                bricks[b, 0:512].astype(F32).reshape(8, 8, 8, 128)
            )
            halves = [
                jnp.dot(
                    spread, bricks[b, 512 + 64 * h : 576 + 64 * h], preferred_element_type=F32
                ).astype(BF16)
                for h in range(2)
            ]
            spaced.append(
                jnp.concatenate(
                    [halves[0][:128], halves[1][:128], halves[0][128:], halves[1][128:]], axis=1
                )
            )
        spaced = jnp.concatenate(spaced, axis=0)
        for ab in range(4):
            made = jnp.dot(spaced, up_weight[ab], preferred_element_type=F32)
            made = made.astype(BF16).astype(F32).reshape(BRICKS, 4, 4, 8, 128)
            for b in range(BRICKS):
                for i in range(4):
                    for j in range(4):
                        pool[
                            group * BRICKS + b, 2 * i + ab // 2, 2 * j + ab % 2, :, 0:128
                        ] = made[b, i, j]
    pool[3 * BRICKS] = jnp.zeros((8, 8, 8, 256), F32)

    spans = {-1: (slice(7, 8), slice(0, 1)), 0: (slice(0, 8), slice(1, 9)), 1: (slice(0, 1), slice(9, 10))}

    @pl.loop(0, BRICKS)
    def _(b):
        for off_x in (-1, 0, 1):
            for off_y in (-1, 0, 1):
                from_x, to_x = spans[off_x]
                from_y, to_y = spans[off_y]
                line = []
                for off_z in (-1, 0, 1):
                    code = (off_x + 1) * 9 + (off_y + 1) * 3 + off_z + 1
                    brick = BRICKS + b if code == 13 else lookup[b * 26 + code - (code > 13)]
                    line.append(pool[brick, from_x, from_y])
                z = lax.broadcasted_iota(I32, line[1].shape, 2)
                shifted[0, to_x, to_y] = pltpu.roll(jnp.where(z == 7, line[0], line[1]), 1, 2)
                shifted[1, to_x, to_y] = line[1]
                shifted[2, to_x, to_y] = pltpu.roll(jnp.where(z == 0, line[2], line[1]), 7, 2)
        for step_y in range(3):
            for step_z in range(3):
                first = (step_y * 3 + step_z) * 256
                window[:, first : first + 256] = (
                    shifted[step_z, :, step_y : step_y + 8].reshape(640, 256).astype(BF16)
                )
        total = jnp.dot(window[0:512], conv_weight[0], preferred_element_type=F32)
        for step_x in (1, 2):
            total += jnp.dot(
                window[64 * step_x : 64 * step_x + 512],
                conv_weight[step_x],
                preferred_element_type=F32,
            )
        out[b] = jnp.maximum(total, 0.0).astype(BF16)


def refine(lookup, before, own, after, up_weight, conv_weight):
    return pl.pallas_call(
        conv_kernel,
        out_shape=jax.ShapeDtypeStruct((BRICKS, 512, 128), BF16),
        in_specs=[SMEM] + [VMEM] * 5,
        out_specs=VMEM,
        scratch_shapes=[
            pltpu.VMEM((3 * BRICKS + 1, 8, 8, 8, 256), F32),
            pltpu.VMEM((3, 10, 10, 8, 256), F32),
            pltpu.VMEM((640, 9 * 256), BF16),
        ],
        compiler_params=pltpu.CompilerParams(vmem_limit_bytes=48 * 2**20),
    )(lookup, before, own, after, up_weight, conv_weight)


def per_device(parents, parent_dest, skip, skip_dest, neighbours, up_weight, conv_weight):
    row, inner = lax.axis_index("gx"), lax.axis_index("gy")
    devices = LINES * COLUMNS
    base = (row * devices * BRICKS).reshape(1)
    place = jnp.stack([inner // COLUMNS, inner % COLUMNS])
    groups = [[x * COLUMNS + q for q in range(COLUMNS)] for x in range(LINES)]
    first = first_pack(parent_dest, skip_dest, base, parents, skip)
    came = lax.all_to_all(first, "gy", 0, 0, tiled=True, axis_index_groups=groups)
    messages = second_pack(place, came)
    arrived = [messages[0]] + [
        lax.ppermute(
            messages[k], "gy", [(i, (i + k * COLUMNS) % devices) for i in range(devices)]
        )
        for k in range(1, LINES)
    ]
    own, flag = unpack(arrived)
    own, _ = lax.while_loop(
        lambda state: state[1][0] > 0,
        lambda state: (
            dense_route(parents, parent_dest, skip, skip_dest),
            jnp.zeros_like(state[1]),
        ),
        (own, flag),
    )
    whole = lax.axis_size(("gx", "gy"))
    up = [(i, i + 1) for i in range(whole - 1)]
    before = lax.ppermute(own, ("gx", "gy"), up)
    after = lax.ppermute(own, ("gx", "gy"), [(j, i) for i, j in up])
    me = row * devices + inner
    lookup = jnp.where(neighbours >= 0, neighbours - (me - 1) * BRICKS, 3 * BRICKS)
    return refine(
        lookup.reshape(-1),
        before,
        own,
        after,
        up_weight.reshape(4, 512, 128),
        conv_weight.reshape(3, 9 * 256, 128),
    )


def solution(mesh):
    placed = (
        P(("gx", "gy"), None, None),
        P(("gx", "gy")),
        P(("gx", "gy"), None, None),
        P(("gx", "gy")),
        P(("gx", "gy"), None),
        P(),
        P(),
    )
    return jax.shard_map(
        per_device,
        mesh=mesh,
        in_specs=placed,
        out_specs=P(("gx", "gy"), None, None),
        check_vma=False,
    )
```

```python
import jax
import jax.numpy as jnp
from jax import lax
from jax.experimental import pallas as pl
from jax.experimental.pallas import tpu as pltpu
from jax.sharding import PartitionSpec as P

LINES, COLUMNS = 4, 8
SLOTS, BRICKS = 8, 4
SKIP_ROWS, PARENT_ROWS, HEAD_ROWS = 512, 128, 16
BODY = SKIP_ROWS + PARENT_ROWS
DEPTH = 2
PIECES = ((SKIP_ROWS, 0, 0), (PARENT_ROWS, SKIP_ROWS, SKIP_ROWS * DEPTH))
BF16, F32, I32 = jnp.bfloat16, jnp.float32, jnp.int32

ANY = pl.BlockSpec(memory_space=pl.ANY)
SMEM = pl.BlockSpec(memory_space=pltpu.SMEM)
VMEM = pl.BlockSpec(memory_space=pltpu.VMEM)


def rows_of(shape, values):
    row = lax.broadcasted_iota(I32, shape, 0)
    out = jnp.full(shape, -1, I32)
    for j, value in enumerate(values):
        out = jnp.where(row == j, value, out)
    return out


def first_kernel(parent_dest, skip_dest, base, parents, skip, out, stage, head, slot_of, sems):
    for q in range(2 * COLUMNS + 1):
        slot_of[q] = 0
    table = []
    for kind, dest in enumerate((skip_dest, parent_dest)):
        for s in range(SLOTS):
            d = dest[s]
            local = jnp.where(d >= 0, d - base[0], -1)
            table.append(local)
            column = lax.rem(lax.div(jnp.maximum(local, 0), BRICKS), COLUMNS)
            slot_of[jnp.where(d >= 0, kind * COLUMNS + column, 2 * COLUMNS)] = s
    head[...] = rows_of((HEAD_ROWS, 128), table).astype(F32).astype(BF16)
    into, onward = [], []
    for q in range(COLUMNS):
        s, p = slot_of[q], slot_of[COLUMNS + q]
        pieces = [(skip.at[s], slice(0, 512))] + [
            (parents.at[p, :, 128 * half : 128 * half + 128], slice(512 + 64 * half, 576 + 64 * half))
            for half in range(2)
        ]
        for j, (source, rows) in enumerate(pieces):
            into.append(pltpu.make_async_copy(source, stage.at[q, rows], sems.at[0, q, j]))
            onward.append(
                pltpu.make_async_copy(stage.at[q, rows], out.at[q, rows], sems.at[1, q, j])
            )
        onward.append(
            pltpu.make_async_copy(head, out.at[q, BODY : BODY + HEAD_ROWS], sems.at[1, q, 3])
        )
    for copy in into:
        copy.start()
    for q in range(COLUMNS):
        onward[4 * q + 3].start()
    for q in range(COLUMNS):
        for j in range(3):
            into[3 * q + j].wait()
            onward[4 * q + j].start()
    for copy in onward:
        copy.wait()


def first_pack(parent_dest, skip_dest, base, parents, skip):
    return pl.pallas_call(
        first_kernel,
        out_shape=jax.ShapeDtypeStruct((COLUMNS, BODY + HEAD_ROWS, 128), BF16),
        in_specs=[SMEM, SMEM, SMEM, ANY, ANY],
        out_specs=ANY,
        scratch_shapes=[
            pltpu.VMEM((COLUMNS, BODY, 128), BF16),
            pltpu.VMEM((HEAD_ROWS, 128), BF16),
            pltpu.SMEM((2 * COLUMNS + 1,), I32),
            pltpu.SemaphoreType.DMA((2, COLUMNS, 4)),
        ],
    )(parent_dest, skip_dest, base, parents, skip)


def second_kernel(place, came, *refs):
    outs = refs[:LINES]
    found, table, counts, source, landing, sem = refs[LINES:]
    line, column = place[0], place[1]
    for j in range(2 * LINES + 1):
        counts[j] = 0
    for j in range(2 * LINES * DEPTH + 1):
        source[j] = 0
        landing[j] = -1
    lane = lax.broadcasted_iota(I32, (COLUMNS, SLOTS, 128), 2)
    over = jnp.zeros((1, 128), I32)
    picks = []
    every = came[:, BODY : BODY + HEAD_ROWS].astype(F32).astype(I32)
    for kind in range(2):
        dest = every[:, kind * SLOTS : kind * SLOTS + SLOTS]
        live = dest >= 0
        owner = dest >> 2
        its_column = owner & 7
        mine = jnp.where(live & (its_column == column), dest, -1)
        picks.append(jnp.max(mine, axis=1))
        to_column = jnp.where(live & (its_column == lane), 1, 0)
        over = over | jnp.where(
            jnp.max(jnp.sum(to_column, axis=1), axis=0, keepdims=True) > 1, 1, 0
        )
        to_owner = jnp.where(live & (owner == lane), 1, 0)
        total = jnp.sum(jnp.sum(to_owner, axis=1), axis=0, keepdims=True)
        over = over | jnp.where(total > DEPTH, 1, 0)
    flag = jnp.max(over.astype(F32), axis=1, keepdims=True).astype(I32)
    lane = lax.broadcasted_iota(I32, (COLUMNS, 128), 1)
    found[...] = jnp.where(lane == 0, picks[0], picks[1])
    copy = pltpu.make_async_copy(found, table, sem)
    copy.start()
    copy.wait()
    for kind in range(2):
        for m in range(COLUMNS):
            dest = table[m, kind]
            live = dest >= 0
            to_line = jnp.where(live, dest >> 5, 0)
            count_at = jnp.where(live, kind * LINES + to_line, 2 * LINES)
            rank = counts[count_at]
            counts[count_at] = rank + 1
            spot = jnp.where(
                live & (rank < DEPTH),
                (kind * LINES + to_line) * DEPTH + rank,
                2 * LINES * DEPTH,
            )
            source[spot] = m
            landing[spot] = dest & 3
    for k in range(LINES):
        to_line = lax.rem(line + k, LINES)
        spots = []
        for kind, (rows, first, height) in enumerate(PIECES):
            for r in range(DEPTH):
                spot = (kind * LINES + to_line) * DEPTH + r
                spots.append(landing[spot])
                outs[k][height + r * rows : height + r * rows + rows] = came[
                    source[spot], first : first + rows
                ]
        outs[k][BODY * DEPTH : BODY * DEPTH + HEAD_ROWS] = (
            rows_of((HEAD_ROWS, 128), spots + [flag]).astype(F32).astype(BF16)
        )


def second_pack(place, came):
    message = jax.ShapeDtypeStruct((BODY * DEPTH + HEAD_ROWS, 128), BF16)
    return pl.pallas_call(
        second_kernel,
        out_shape=[message] * LINES,
        in_specs=[SMEM, VMEM],
        out_specs=[VMEM] * LINES,
        scratch_shapes=[
            pltpu.VMEM((COLUMNS, 128), I32),
            pltpu.SMEM((COLUMNS, 128), I32),
            pltpu.SMEM((2 * LINES + 1,), I32),
            pltpu.SMEM((2 * LINES * DEPTH + 1,), I32),
            pltpu.SMEM((2 * LINES * DEPTH + 1,), I32),
            pltpu.SemaphoreType.DMA,
        ],
        compiler_params=pltpu.CompilerParams(vmem_limit_bytes=16 * 2**20),
    )(place, came)


def unpack_kernel(*refs):
    came = refs[:LINES]
    own, flag_out, found, table, sem = refs[LINES:]
    lane = lax.broadcasted_iota(I32, (HEAD_ROWS, 128), 1)
    row = lax.broadcasted_iota(I32, (HEAD_ROWS, 128), 0)
    for k in range(LINES):
        header = came[k][BODY * DEPTH : BODY * DEPTH + HEAD_ROWS].astype(F32)
        found[k : k + 1] = jnp.sum(
            jnp.where(lane == row, header, 0.0), axis=0, keepdims=True
        ).astype(I32)
    found[LINES:8] = jnp.zeros((8 - LINES, 128), I32)
    copy = pltpu.make_async_copy(found, table, sem)
    copy.start()
    copy.wait()
    flag = table[0, 2 * DEPTH]
    for k in range(1, LINES):
        flag = flag | table[k, 2 * DEPTH]
    flag_out[0] = flag
    for k in range(LINES):
        for kind, (rows, first, height) in enumerate(PIECES):
            for r in range(DEPTH):
                brick = table[k, kind * DEPTH + r]

                @pl.when(brick >= 0)
                def _(k=k, rows=rows, first=first, at=height + r * rows, brick=brick):
                    own[brick, first : first + rows] = came[k][at : at + rows]


def unpack(messages):
    return pl.pallas_call(
        unpack_kernel,
        out_shape=[
            jax.ShapeDtypeStruct((BRICKS, BODY, 128), BF16),
            jax.ShapeDtypeStruct((1,), I32),
        ],
        in_specs=[VMEM] * LINES,
        out_specs=[VMEM, SMEM],
        scratch_shapes=[
            pltpu.VMEM((8, 128), I32),
            pltpu.SMEM((8, 128), I32),
            pltpu.SemaphoreType.DMA,
        ],
        compiler_params=pltpu.CompilerParams(vmem_limit_bytes=16 * 2**20),
    )(*messages)


def dense_pack_kernel(parent_dest, skip_dest, base, parents, skip, out, head, sems, sem):
    table = []
    copies = []
    for kind, dest in enumerate((skip_dest, parent_dest)):
        for s in range(SLOTS):
            local = jnp.where(dest[s] >= 0, dest[s] - base[0], -1)
            table.append(local)
            owner = lax.div(jnp.maximum(local, 0), BRICKS)
            if kind == 0:
                pieces = [(skip.at[s], out.at[owner, 0:512])]
            else:
                pieces = [
                    (
                        parents.at[s, :, 128 * half : 128 * half + 128],
                        out.at[owner, 512 + 64 * half : 576 + 64 * half],
                    )
                    for half in range(2)
                ]
            for j, (source, target) in enumerate(pieces):
                copies.append(
                    (local, pltpu.make_async_copy(source, target, sems.at[s, kind + j]))
                )
    head[...] = rows_of((HEAD_ROWS, 128), table).astype(F32).astype(BF16)
    for live, copy in copies:
        pl.when(live >= 0)(copy.start)
    for owner in range(LINES * COLUMNS):
        copy = pltpu.make_async_copy(head, out.at[owner, BODY : BODY + HEAD_ROWS], sem)
        copy.start()
        copy.wait()
    for live, copy in copies:
        pl.when(live >= 0)(copy.wait)


def dense_unpack_kernel(place, came, own, heads, found, table, sems, sem):
    devices = LINES * COLUMNS
    copy = pltpu.make_async_copy(came.at[:, BODY : BODY + HEAD_ROWS], heads, sem)
    copy.start()
    copy.wait()
    me = place[0] * COLUMNS + place[1]
    picks = []
    for kind in range(2):
        dest = heads[:, kind * SLOTS : kind * SLOTS + SLOTS].astype(F32).astype(I32)
        mine = jnp.where((dest >= 0) & ((dest >> 2) == me), dest, -1)
        picks.append(jnp.max(mine, axis=1))
    lane = lax.broadcasted_iota(I32, (devices, 128), 1)
    found[...] = jnp.where(lane == 0, picks[0], picks[1])
    copy = pltpu.make_async_copy(found, table, sem)
    copy.start()
    copy.wait()
    for m in range(devices):
        for kind, (rows, first, _) in enumerate(PIECES):
            dest = table[m, kind]
            copy = pltpu.make_async_copy(
                came.at[m, first : first + rows],
                own.at[jnp.maximum(dest, 0) & 3, first : first + rows],
                sems.at[kind],
            )

            @pl.when(dest >= 0)
            def _(copy=copy):
                copy.start()
                copy.wait()


def dense_route(place, base, parents, parent_dest, skip, skip_dest):
    devices = LINES * COLUMNS
    limit = pltpu.CompilerParams(vmem_limit_bytes=16 * 2**20)
    rows = pl.pallas_call(
        dense_pack_kernel,
        out_shape=jax.ShapeDtypeStruct((devices, BODY + HEAD_ROWS, 128), BF16),
        in_specs=[SMEM, SMEM, SMEM, ANY, ANY],
        out_specs=ANY,
        scratch_shapes=[
            pltpu.VMEM((HEAD_ROWS, 128), BF16),
            pltpu.SemaphoreType.DMA((SLOTS, 3)),
            pltpu.SemaphoreType.DMA,
        ],
        compiler_params=limit,
    )(parent_dest, skip_dest, base, parents, skip)
    came = lax.all_to_all(rows, "gy", 0, 0, tiled=True)
    return pl.pallas_call(
        dense_unpack_kernel,
        out_shape=jax.ShapeDtypeStruct((BRICKS, BODY, 128), BF16),
        in_specs=[SMEM, ANY],
        out_specs=VMEM,
        scratch_shapes=[
            pltpu.VMEM((devices, HEAD_ROWS, 128), BF16),
            pltpu.VMEM((devices, 128), I32),
            pltpu.SMEM((devices, 128), I32),
            pltpu.SemaphoreType.DMA((2,)),
            pltpu.SemaphoreType.DMA,
        ],
        compiler_params=limit,
    )(place, came)


def fill_pool(pool, groups, up_weight):
    row = lax.broadcasted_iota(I32, (256, 64), 0)
    column = lax.broadcasted_iota(I32, (256, 64), 1)
    in_brick = row & 127
    takes = (in_brick >> 3) * 4 + ((in_brick & 7) >> 1) == column
    spread = jnp.where(takes & ((row & 1) == (row >> 7)), 1.0, 0.0).astype(BF16)
    for group, bricks in enumerate(groups):
        spaced = []
        for b in range(BRICKS):
            pool[group * BRICKS + b, 1] = bricks[b, 0:512].astype(F32)
            halves = [
                jnp.dot(
                    spread, bricks[b, 512 + 64 * h : 576 + 64 * h], preferred_element_type=F32
                ).astype(BF16)
                for h in range(2)
            ]
            spaced.append(
                jnp.concatenate(
                    [halves[0][:128], halves[1][:128], halves[0][128:], halves[1][128:]], axis=1
                )
            )
        spaced = jnp.concatenate(spaced, axis=0)
        for ab in range(4):
            made = jnp.dot(spaced, up_weight[ab], preferred_element_type=F32)
            made = made.astype(BF16).astype(F32)
            for b in range(BRICKS):
                for i in range(4):
                    for j in range(4):
                        first = (2 * i + ab // 2) * 64 + (2 * j + ab % 2) * 8
                        came = b * 128 + i * 32 + j * 8
                        pool[group * BRICKS + b, 0, first : first + 8] = made[came : came + 8]
    pool[len(groups) * BRICKS] = jnp.zeros((2, 512, 128), F32)


def rows_from(pool, brick, rows):
    return jnp.concatenate([pool[brick, 0, rows], pool[brick, 1, rows]], axis=1)


def shift_rows(line):
    z = lax.broadcasted_iota(I32, line[1].shape, 1)
    return (
        pltpu.roll(jnp.where(z == 7, line[0], line[1]), 1, 1),
        line[1],
        pltpu.roll(jnp.where(z == 0, line[2], line[1]), 7, 1),
    )


def code_of(off_x, off_y, off_z):
    code = (off_x + 1) * 9 + (off_y + 1) * 3 + off_z + 1
    return code - (code > 13)


def near_kernel(
    lookup, own, up_weight, pair_weight, last_weight, out, pool, shifted_pair, window_pair
):
    fill_pool(pool, (own,), up_weight)
    spans = {-1: (7, 8, 0), 0: (0, 8, 1), 1: (0, 1, 9)}

    for b in range(BRICKS):
        shifted, window = shifted_pair[b % 2], window_pair[b % 2]
        for off_x in (-1, 0, 1):
            for off_y in (-1, 0, 1):
                low_x, high_x, to_x = spans[off_x]
                low_y, high_y, to_y = spans[off_y]
                deep = high_y - low_y
                bricks = [
                    b if off_x == off_y == off_z == 0 else lookup[b * 26 + code_of(off_x, off_y, off_z)]
                    for off_z in (-1, 0, 1)
                ]
                for x in range(low_x, high_x):
                    first = x * 64 + low_y * 8
                    line = [
                        rows_from(pool, brick, pl.ds(first, deep * 8)).reshape(deep, 8, 256)
                        for brick in bricks
                    ]
                    for step, rows in enumerate(shift_rows(line)):
                        shifted[step, to_x + x - low_x, to_y : to_y + deep] = rows
        for step_y in range(3):
            for step_z in range(3):
                first = (step_y * 3 + step_z) * 256
                window[:, first : first + 256] = (
                    shifted[step_z, :, step_y : step_y + 8].reshape(640, 256).astype(BF16)
                )
        pair = jnp.dot(window[0:576], pair_weight[...], preferred_element_type=F32)
        last = jnp.dot(window[128:640], last_weight[...], preferred_element_type=F32)
        out[b] = pair[0:512, 0:128] + pair[64:576, 128:256] + last


def far_kernel(
    lookup, before, after, near, up_weight, conv_weight, out, pool, shifted, window, total
):
    fill_pool(pool, (before, after), up_weight)
    total[...] = near[...].reshape(BRICKS * 512, 128)
    shifted[...] = jnp.zeros(shifted.shape, F32)

    @pl.loop(0, BRICKS)
    def _(b):
        def brick(*offsets):
            return lookup[b * 26 + code_of(*offsets)]

        def keep(side):
            for step in range(3):
                for inner in range(3):
                    first = (step * 3 + inner) * 256
                    window[side, pl.ds(pl.multiple_of(b * 64, 64), 64), first : first + 256] = (
                        shifted[side, inner, step : step + 8].reshape(64, 256).astype(BF16)
                    )

        for side, off in enumerate((-1, 1)):
            edge = 7 if off < 0 else 0
            for off_y in (-1, 0, 1):
                bricks = [brick(off, off_y, off_z) for off_z in (-1, 0, 1)]
                low, deep, to = ((7, 1, 0), (0, 8, 1), (0, 1, 9))[off_y + 1]
                first = edge * 64 + low * 8
                line = [
                    rows_from(pool, n, pl.ds(first, deep * 8)).reshape(deep, 8, 256)
                    for n in bricks
                ]
                for step, rows in enumerate(shift_rows(line)):
                    shifted[side, step, to : to + deep] = rows
            keep(side)
            bricks = [brick(0, off, off_z) for off_z in (-1, 0, 1)]
            for x in range(8):
                first = x * 64 + edge * 8
                line = [rows_from(pool, n, pl.ds(first, 8)).reshape(1, 8, 256) for n in bricks]
                for step, rows in enumerate(shift_rows(line)):
                    shifted[2 + side, step, 1 + x : 2 + x] = rows
            keep(2 + side)
            face = rows_from(pool, brick(0, 0, off), pl.ds(edge, 64, stride=8)).reshape(8, 8, 256)
            y = lax.broadcasted_iota(I32, face.shape, 1)
            shifted[4 + side, 0, 1:9] = jnp.where(y == 0, 0.0, pltpu.roll(face, 1, 1))
            shifted[4 + side, 1, 1:9] = face
            shifted[4 + side, 2, 1:9] = jnp.where(y == 7, 0.0, pltpu.roll(face, 7, 1))
            keep(4 + side)

    for side in range(2):
        tap = 2 * side
        added = jnp.dot(window[side], conv_weight[tap], preferred_element_type=F32)
        for b in range(BRICKS):
            first = b * 512 + 448 * side
            total[first : first + 64] += added[b * 64 : b * 64 + 64]
        added = jnp.zeros((256, 128), F32)
        for x in range(3):
            added += jnp.dot(
                window[2 + side, :, x * 768 : x * 768 + 768],
                conv_weight[x, tap * 768 : tap * 768 + 768],
                preferred_element_type=F32,
            )
        for r in range(BRICKS * 8):
            first = r * 64 + 56 * side
            total[first : first + 8] += added[r * 8 : r * 8 + 8]
        added = jnp.zeros((256, 128), F32)
        for x in range(3):
            for y in range(3):
                added += jnp.dot(
                    window[4 + side, :, (x * 3 + y) * 256 : (x * 3 + y) * 256 + 256],
                    conv_weight[x, (y * 3 + tap) * 256 : (y * 3 + tap) * 256 + 256],
                    preferred_element_type=F32,
                )
        at = pl.ds(7 * side, BRICKS * 64, stride=8)
        total[at] = total[at] + added
    out[...] = jnp.maximum(total[...], 0.0).astype(BF16).reshape(BRICKS, 512, 128)


def convolve_near(lookup, own, up_weight, pair_weight, last_weight):
    return pl.pallas_call(
        near_kernel,
        out_shape=jax.ShapeDtypeStruct((BRICKS, 512, 128), F32),
        in_specs=[SMEM] + [VMEM] * 4,
        out_specs=VMEM,
        scratch_shapes=[
            pltpu.VMEM((BRICKS + 1, 2, 512, 128), F32),
            [pltpu.VMEM((3, 10, 10, 8, 256), F32)] * 2,
            [pltpu.VMEM((640, 9 * 256), BF16)] * 2,
        ],
        compiler_params=pltpu.CompilerParams(vmem_limit_bytes=32 * 2**20),
        cost_estimate=pl.CostEstimate(
            flops=10**10, bytes_accessed=4 * 10**7, transcendentals=0
        ),
    )(lookup, own, up_weight, pair_weight, last_weight)


def convolve_far(lookup, before, after, near, up_weight, conv_weight):
    return pl.pallas_call(
        far_kernel,
        out_shape=jax.ShapeDtypeStruct((BRICKS, 512, 128), BF16),
        in_specs=[SMEM] + [VMEM] * 5,
        out_specs=VMEM,
        scratch_shapes=[
            pltpu.VMEM((2 * BRICKS + 1, 2, 512, 128), F32),
            pltpu.VMEM((6, 3, 10, 8, 256), F32),
            pltpu.VMEM((6, BRICKS * 64, 9 * 256), BF16),
            pltpu.VMEM((BRICKS * 512, 128), F32),
        ],
        compiler_params=pltpu.CompilerParams(vmem_limit_bytes=32 * 2**20),
    )(lookup, before, after, near, up_weight, conv_weight)


def per_device(parents, parent_dest, skip, skip_dest, neighbours, up_weight, conv_weight):
    row, inner = lax.axis_index("gx"), lax.axis_index("gy")
    devices = LINES * COLUMNS
    base = (row * devices * BRICKS).reshape(1)
    place = jnp.stack([inner // COLUMNS, inner % COLUMNS])
    groups = [[x * COLUMNS + q for q in range(COLUMNS)] for x in range(LINES)]
    first = first_pack(parent_dest, skip_dest, base, parents, skip)
    came = lax.all_to_all(first, "gy", 0, 0, tiled=True, axis_index_groups=groups)
    messages = second_pack(place, came)
    arrived = [messages[0]] + [
        lax.ppermute(
            messages[k], "gy", [(i, (i + k * COLUMNS) % devices) for i in range(devices)]
        )
        for k in range(1, LINES)
    ]
    own, flag = unpack(arrived)
    own, _ = lax.while_loop(
        lambda state: state[1][0] > 0,
        lambda state: (
            dense_route(place, base, parents, parent_dest, skip, skip_dest),
            jnp.zeros_like(state[1]),
        ),
        (own, flag),
    )
    whole = lax.axis_size(("gx", "gy"))
    up = [(i, i + 1) for i in range(whole - 1)]
    before = lax.ppermute(own, ("gx", "gy"), up)
    after = lax.ppermute(own, ("gx", "gy"), [(j, i) for i, j in up])
    me = row * devices + inner
    ahead = neighbours - me * BRICKS
    here = (neighbours >= 0) & (ahead >= 0) & (ahead < BRICKS)
    near_lookup = jnp.where(here, ahead, BRICKS)
    far = jnp.where(ahead < 0, ahead + BRICKS, ahead)
    far_lookup = jnp.where((neighbours >= 0) & ~here, far, 2 * BRICKS)
    up_weight = up_weight.reshape(4, 512, 128)
    conv_weight = conv_weight.reshape(3, 9 * 256, 128)
    pair_weight = jnp.concatenate([conv_weight[0], conv_weight[1]], axis=1)
    near = convolve_near(
        near_lookup.reshape(-1), own, up_weight, pair_weight, conv_weight[2]
    )
    return convolve_far(far_lookup.reshape(-1), before, after, near, up_weight, conv_weight)


def solution(mesh):
    placed = (
        P(("gx", "gy"), None, None),
        P(("gx", "gy")),
        P(("gx", "gy"), None, None),
        P(("gx", "gy")),
        P(("gx", "gy"), None),
        P(),
        P(),
    )
    return jax.shard_map(
        per_device,
        mesh=mesh,
        in_specs=placed,
        out_specs=P(("gx", "gy"), None, None),
        check_vma=False,
    )
```

```python
import jax
import jax.numpy as jnp
from jax import lax
from jax.experimental import pallas as pl
from jax.experimental.pallas import tpu as pltpu
from jax.sharding import PartitionSpec as P

LINES, COLUMNS = 4, 8
SLOTS, BRICKS = 8, 4
SKIP_ROWS, PARENT_ROWS, HEAD_ROWS = 512, 128, 16
BODY = SKIP_ROWS + PARENT_ROWS
DEPTH = 2
PIECES = ((SKIP_ROWS, 0, 0), (PARENT_ROWS, SKIP_ROWS, SKIP_ROWS * DEPTH))
BF16, F32, I32 = jnp.bfloat16, jnp.float32, jnp.int32

ANY = pl.BlockSpec(memory_space=pl.ANY)
SMEM = pl.BlockSpec(memory_space=pltpu.SMEM)
VMEM = pl.BlockSpec(memory_space=pltpu.VMEM)


def rows_of(shape, values):
    row = lax.broadcasted_iota(I32, shape, 0)
    out = jnp.full(shape, -1, I32)
    for j, value in enumerate(values):
        out = jnp.where(row == j, value, out)
    return out


WAYS = ((0, 0), (0, 1), (1, 0), (3, 0), (2, 0), (2, 1), (1, 1), (3, 1))


def column_at(column, j):
    along, other = WAYS[j]
    return ((column + 2 * along) & 6) | ((column ^ other) & 1)


def first_kernel(parent_dest, skip_dest, place, parents, skip, *refs):
    outs = refs[:COLUMNS]
    slot_of, sems = refs[COLUMNS:]
    for q in range(2 * COLUMNS + 1):
        slot_of[q] = 0
    table = []
    for kind, dest in enumerate((skip_dest, parent_dest)):
        for s in range(SLOTS):
            d = dest[s]
            local = jnp.where(d >= 0, d - place[2], -1)
            table.append(local)
            column = (local >> 2) & 7
            slot_of[jnp.where(d >= 0, kind * COLUMNS + column, 2 * COLUMNS)] = s
    copies = []
    for j in range(COLUMNS):
        q = column_at(place[1], j)
        s, p = slot_of[q], slot_of[COLUMNS + q]
        copies.append(pltpu.make_async_copy(skip.at[s], outs[j].at[0:512], sems.at[j, 0]))
        for half in range(2):
            copies.append(
                pltpu.make_async_copy(
                    parents.at[p, :, 128 * half : 128 * half + 128],
                    outs[j].at[512 + 64 * half : 576 + 64 * half],
                    sems.at[j, 1 + half],
                )
            )
    for copy in copies:
        copy.start()
    head = rows_of((HEAD_ROWS, 128), table).astype(F32).astype(BF16)
    for j in range(COLUMNS):
        outs[j][BODY : BODY + HEAD_ROWS] = head
    for copy in copies:
        copy.wait()


def first_pack(parent_dest, skip_dest, place, parents, skip):
    return pl.pallas_call(
        first_kernel,
        out_shape=[jax.ShapeDtypeStruct((BODY + HEAD_ROWS, 128), BF16)] * COLUMNS,
        in_specs=[SMEM, SMEM, SMEM, ANY, ANY],
        out_specs=[VMEM] * COLUMNS,
        scratch_shapes=[
            pltpu.SMEM((2 * COLUMNS + 1,), I32),
            pltpu.SemaphoreType.DMA((COLUMNS, 3)),
        ],
        compiler_params=pltpu.CompilerParams(vmem_limit_bytes=FIRST_LIMIT),
    )(parent_dest, skip_dest, place, parents, skip)


FIRST_LIMIT = 16 * 2**20


HOPS = (0, 2, 1, 3)


def second_kernel(place, *refs):
    came, outs = refs[:COLUMNS], refs[COLUMNS : COLUMNS + LINES]
    found, table, counts, landing, sem = refs[COLUMNS + LINES :]
    line, column = place[0], place[1]
    over = jnp.zeros((1, 128), I32)
    totals = [jnp.zeros((1, 128), I32)] * 2
    row = lax.broadcasted_iota(I32, (SLOTS, 128), 0)
    lane = lax.broadcasted_iota(I32, (SLOTS, 128), 1)
    picks = jnp.full((SLOTS, 128), -1, I32)
    for m in range(COLUMNS):
        every = came[m][BODY : BODY + HEAD_ROWS].astype(F32).astype(I32)
        for kind in range(2):
            dest = every[kind * SLOTS : kind * SLOTS + SLOTS]
            live = dest >= 0
            owner = dest >> 2
            its_column = owner & 7
            mine = jnp.where(live & (its_column == column), dest, -1)
            picks = jnp.where(
                (row == m) & (lane == kind), jnp.max(mine, axis=0, keepdims=True), picks
            )
            to_column = jnp.where(live & (its_column == lane), 1, 0)
            over = over | jnp.where(jnp.sum(to_column, axis=0, keepdims=True) > 1, 1, 0)
            to_owner = jnp.where(live & (owner == lane), 1, 0)
            totals[kind] = totals[kind] + jnp.sum(to_owner, axis=0, keepdims=True)
    found[...] = picks
    copy = pltpu.make_async_copy(found, table, sem)
    copy.start()
    for j in range(2 * LINES + 1):
        counts[j] = 0
    for j in range(2 * LINES * DEPTH + 1):
        landing[j] = -1
    for kind in range(2):
        over = over | jnp.where(totals[kind] > DEPTH, 1, 0)
    flag = jnp.max(over.astype(F32), axis=1, keepdims=True).astype(I32)
    copy.wait()
    for m in range(COLUMNS):
        for kind, (rows, first, height) in enumerate(PIECES):
            dest = table[m, kind]
            live = dest >= 0
            ahead = ((dest >> 5) - line) & 3
            count_at = jnp.where(live, kind * LINES + ahead, 2 * LINES)
            rank = counts[count_at]
            counts[count_at] = rank + 1
            fits = live & (rank < DEPTH)
            spot = (kind * LINES + ahead) * DEPTH + rank
            landing[jnp.where(fits, spot, 2 * LINES * DEPTH)] = dest & 3
            at = pl.multiple_of(height + jnp.where(fits, rank, 0) * rows, 128)
            for k in range(LINES):

                @pl.when(fits & (ahead == HOPS[k]))
                def _(m=m, k=k, rows=rows, first=first, at=at):
                    outs[k][pl.ds(at, rows)] = came[m][first : first + rows]

    for k in range(LINES):
        spots = [
            landing[(kind * LINES + HOPS[k]) * DEPTH + r]
            for kind in range(2) for r in range(DEPTH)
        ]
        outs[k][BODY * DEPTH : BODY * DEPTH + HEAD_ROWS] = (
            rows_of((HEAD_ROWS, 128), spots + [flag]).astype(F32).astype(BF16)
        )


def second_pack(place, came):
    message = jax.ShapeDtypeStruct((BODY * DEPTH + HEAD_ROWS, 128), BF16)
    return pl.pallas_call(
        second_kernel,
        out_shape=[message] * LINES,
        in_specs=[SMEM] + [VMEM] * COLUMNS,
        out_specs=[VMEM] * LINES,
        scratch_shapes=[
            pltpu.VMEM((COLUMNS, 128), I32),
            pltpu.SMEM((COLUMNS, 128), I32),
            pltpu.SMEM((2 * LINES + 1,), I32),
            pltpu.SMEM((2 * LINES * DEPTH + 1,), I32),
            pltpu.SemaphoreType.DMA,
        ],
        compiler_params=pltpu.CompilerParams(vmem_limit_bytes=16 * 2**20),
    )(place, *came)


SURFACE = 352


def keep_surface(own, surface, plain):
    for b in range(BRICKS):
        plain[...] = own[b, 0:SKIP_ROWS].astype(F32)
        surface[b, 0:64] = own[b, 0:64]
        surface[b, 64:128] = own[b, 448:512]
        for side in range(2):
            lines = [
                plain[x * 64 + 56 * side : x * 64 + 56 * side + 8] for x in range(1, 7)
            ]
            surface[b, 128 + 48 * side : 176 + 48 * side] = jnp.concatenate(lines).astype(BF16)
            surface[b, 224 + 64 * side : 288 + 64 * side] = plain[
                pl.ds(7 * side, 64, stride=8)
            ].astype(BF16)
        surface[b, SURFACE : SURFACE + PARENT_ROWS] = own[b, SKIP_ROWS:BODY]


def unpack_kernel(*refs):
    came = refs[:LINES]
    own, surface, flag_out, plain, found, table, sem = refs[LINES:]
    lane = lax.broadcasted_iota(I32, (HEAD_ROWS, 128), 1)
    row = lax.broadcasted_iota(I32, (HEAD_ROWS, 128), 0)
    for k in range(LINES):
        header = came[k][BODY * DEPTH : BODY * DEPTH + HEAD_ROWS].astype(F32)
        found[k : k + 1] = jnp.sum(
            jnp.where(lane == row, header, 0.0), axis=0, keepdims=True
        ).astype(I32)
    found[LINES:8] = jnp.zeros((8 - LINES, 128), I32)
    copy = pltpu.make_async_copy(found, table, sem)
    copy.start()
    copy.wait()
    flag = table[0, 2 * DEPTH]
    for k in range(1, LINES):
        flag = flag | table[k, 2 * DEPTH]
    flag_out[0] = flag
    for k in range(LINES):
        for kind, (rows, first, height) in enumerate(PIECES):
            for r in range(DEPTH):
                brick = table[k, kind * DEPTH + r]

                @pl.when(brick >= 0)
                def _(k=k, rows=rows, first=first, at=height + r * rows, brick=brick):
                    own[brick, first : first + rows] = came[k][at : at + rows]

    keep_surface(own, surface, plain)


def unpack(messages):
    return pl.pallas_call(
        unpack_kernel,
        out_shape=[
            jax.ShapeDtypeStruct((BRICKS, BODY, 128), BF16),
            jax.ShapeDtypeStruct((BRICKS, SURFACE + PARENT_ROWS, 128), BF16),
            jax.ShapeDtypeStruct((1,), I32),
        ],
        in_specs=[VMEM] * LINES,
        out_specs=[VMEM, VMEM, SMEM],
        scratch_shapes=[
            pltpu.VMEM((SKIP_ROWS, 128), F32),
            pltpu.VMEM((8, 128), I32),
            pltpu.SMEM((8, 128), I32),
            pltpu.SemaphoreType.DMA,
        ],
        compiler_params=pltpu.CompilerParams(vmem_limit_bytes=16 * 2**20),
    )(*messages)


def dense_pack_kernel(parent_dest, skip_dest, place, parents, skip, out, head, sems, sem):
    table = []
    copies = []
    for kind, dest in enumerate((skip_dest, parent_dest)):
        for s in range(SLOTS):
            local = jnp.where(dest[s] >= 0, dest[s] - place[2], -1)
            table.append(local)
            owner = lax.div(jnp.maximum(local, 0), BRICKS)
            if kind == 0:
                pieces = [(skip.at[s], out.at[owner, 0:512])]
            else:
                pieces = [
                    (
                        parents.at[s, :, 128 * half : 128 * half + 128],
                        out.at[owner, 512 + 64 * half : 576 + 64 * half],
                    )
                    for half in range(2)
                ]
            for j, (source, target) in enumerate(pieces):
                copies.append(
                    (local, pltpu.make_async_copy(source, target, sems.at[s, kind + j]))
                )
    head[...] = rows_of((HEAD_ROWS, 128), table).astype(F32).astype(BF16)
    for live, copy in copies:
        pl.when(live >= 0)(copy.start)
    for owner in range(LINES * COLUMNS):
        copy = pltpu.make_async_copy(head, out.at[owner, BODY : BODY + HEAD_ROWS], sem)
        copy.start()
        copy.wait()
    for live, copy in copies:
        pl.when(live >= 0)(copy.wait)


def dense_unpack_kernel(place, came, own, surface, plain, heads, found, table, sems, sem):
    devices = LINES * COLUMNS
    copy = pltpu.make_async_copy(came.at[:, BODY : BODY + HEAD_ROWS], heads, sem)
    copy.start()
    copy.wait()
    me = place[0] * COLUMNS + place[1]
    picks = []
    for kind in range(2):
        dest = heads[:, kind * SLOTS : kind * SLOTS + SLOTS].astype(F32).astype(I32)
        mine = jnp.where((dest >= 0) & ((dest >> 2) == me), dest, -1)
        picks.append(jnp.max(mine, axis=1))
    lane = lax.broadcasted_iota(I32, (devices, 128), 1)
    found[...] = jnp.where(lane == 0, picks[0], picks[1])
    copy = pltpu.make_async_copy(found, table, sem)
    copy.start()
    copy.wait()
    for m in range(devices):
        for kind, (rows, first, _) in enumerate(PIECES):
            dest = table[m, kind]
            copy = pltpu.make_async_copy(
                came.at[m, first : first + rows],
                own.at[jnp.maximum(dest, 0) & 3, first : first + rows],
                sems.at[kind],
            )

            @pl.when(dest >= 0)
            def _(copy=copy):
                copy.start()
                copy.wait()

    keep_surface(own, surface, plain)


def dense_route(place, parents, parent_dest, skip, skip_dest):
    devices = LINES * COLUMNS
    limit = pltpu.CompilerParams(vmem_limit_bytes=16 * 2**20)
    rows = pl.pallas_call(
        dense_pack_kernel,
        out_shape=jax.ShapeDtypeStruct((devices, BODY + HEAD_ROWS, 128), BF16),
        in_specs=[SMEM, SMEM, SMEM, ANY, ANY],
        out_specs=ANY,
        scratch_shapes=[
            pltpu.VMEM((HEAD_ROWS, 128), BF16),
            pltpu.SemaphoreType.DMA((SLOTS, 3)),
            pltpu.SemaphoreType.DMA,
        ],
        compiler_params=limit,
    )(parent_dest, skip_dest, place, parents, skip)
    came = lax.all_to_all(rows, "gy", 0, 0, tiled=True)
    return pl.pallas_call(
        dense_unpack_kernel,
        out_shape=[
            jax.ShapeDtypeStruct((BRICKS, BODY, 128), BF16),
            jax.ShapeDtypeStruct((BRICKS, SURFACE + PARENT_ROWS, 128), BF16),
        ],
        in_specs=[SMEM, ANY],
        out_specs=[VMEM, VMEM],
        scratch_shapes=[
            pltpu.VMEM((SKIP_ROWS, 128), F32),
            pltpu.VMEM((devices, HEAD_ROWS, 128), BF16),
            pltpu.VMEM((devices, 128), I32),
            pltpu.SMEM((devices, 128), I32),
            pltpu.SemaphoreType.DMA((2,)),
            pltpu.SemaphoreType.DMA,
        ],
        compiler_params=limit,
    )(place, came)


def fill_pool(pool, groups, up_weight, parents_at):
    row = lax.broadcasted_iota(I32, (256, 64), 0)
    column = lax.broadcasted_iota(I32, (256, 64), 1)
    in_brick = row & 127
    takes = (in_brick >> 3) * 4 + ((in_brick & 7) >> 1) == column
    spread = jnp.where(takes & ((row & 1) == (row >> 7)), 1.0, 0.0).astype(BF16)
    for group, bricks in enumerate(groups):
        spaced = []
        for b in range(BRICKS):
            into = pool.at[group * BRICKS + b, 1]
            if parents_at == SKIP_ROWS:
                into[...] = bricks[b, 0:SKIP_ROWS].astype(F32)
            else:
                into[0:64] = bricks[b, 0:64].astype(F32)
                into[448:512] = bricks[b, 64:128].astype(F32)
                for side in range(2):
                    lines = bricks[b, 128 + 48 * side : 176 + 48 * side].astype(F32)
                    for x in range(1, 7):
                        first = x * 64 + 56 * side
                        into[first : first + 8] = lines[x * 8 - 8 : x * 8]
                    pool[group * BRICKS + b, 1, pl.ds(7 * side, 64, stride=8)] = bricks[
                        b, 224 + 64 * side : 288 + 64 * side
                    ].astype(F32)
            halves = [
                jnp.dot(
                    spread,
                    bricks[b, parents_at + 64 * h : parents_at + 64 * h + 64],
                    preferred_element_type=F32,
                ).astype(BF16)
                for h in range(2)
            ]
            spaced.append(
                jnp.concatenate(
                    [halves[0][:128], halves[1][:128], halves[0][128:], halves[1][128:]], axis=1
                )
            )
        spaced = jnp.concatenate(spaced, axis=0)
        every = jnp.dot(spaced, up_weight[...], preferred_element_type=F32)
        every = every.astype(BF16).astype(F32)
        for ab in range(4):
            made = every[:, ab * 128 : ab * 128 + 128]
            for b in range(BRICKS):
                for i in range(4):
                    for j in range(4):
                        first = (2 * i + ab // 2) * 64 + (2 * j + ab % 2) * 8
                        came = b * 128 + i * 32 + j * 8
                        pool[group * BRICKS + b, 0, first : first + 8] = made[came : came + 8]
    pool[len(groups) * BRICKS] = jnp.zeros((2, 512, 128), F32)


def rows_from(pool, brick, rows):
    return jnp.concatenate([pool[brick, 0, rows], pool[brick, 1, rows]], axis=1)


def shift_rows(line):
    z = lax.broadcasted_iota(I32, line[1].shape, 1)
    return (
        pltpu.roll(jnp.where(z == 7, line[0], line[1]), 1, 1),
        line[1],
        pltpu.roll(jnp.where(z == 0, line[2], line[1]), 7, 1),
    )


def code_of(off_x, off_y, off_z):
    code = (off_x + 1) * 9 + (off_y + 1) * 3 + off_z + 1
    return code - (code > 13)


def near_kernel(
    lookup, own, up_weight, pair_weight, conv_weight, out, pool, shifted_pair, window_pair
):
    fill_pool(pool, (own,), up_weight, SKIP_ROWS)
    spans = {-1: (7, 8, 0), 0: (0, 8, 1), 1: (0, 1, 9)}

    for b in range(BRICKS):
        shifted, window = shifted_pair[b % 2], window_pair[b % 2]
        for off_x in (-1, 0, 1):
            for off_y in (-1, 0, 1):
                low_x, high_x, to_x = spans[off_x]
                low_y, high_y, to_y = spans[off_y]
                deep = high_y - low_y
                bricks = [
                    b if off_x == off_y == off_z == 0 else lookup[b * 26 + code_of(off_x, off_y, off_z)]
                    for off_z in (-1, 0, 1)
                ]
                for x in range(low_x, high_x):
                    first = x * 64 + low_y * 8
                    line = [
                        rows_from(pool, brick, pl.ds(first, deep * 8)).reshape(deep, 8, 256)
                        for brick in bricks
                    ]
                    for step, rows in enumerate(shift_rows(line)):
                        shifted[step, to_x + x - low_x, to_y : to_y + deep] = rows
        for step_y in range(3):
            for step_z in range(3):
                first = (step_y * 3 + step_z) * 256
                window[:, first : first + 256] = (
                    shifted[step_z, :, step_y : step_y + 8].reshape(640, 256).astype(BF16)
                )
        pair = jnp.dot(window[0:576], pair_weight[...], preferred_element_type=F32)
        last = jnp.dot(window[128:640], conv_weight[2], preferred_element_type=F32)
        out[b] = pair[0:512, 0:128] + pair[64:576, 128:256] + last


def far_kernel(
    lookup, before, after, near, up_weight, conv_weight, out, pool, shifted, window, total
):
    fill_pool(pool, (before, after), up_weight, SURFACE)
    total[...] = near[...].reshape(BRICKS * 512, 128)
    shifted[...] = jnp.zeros(shifted.shape, F32)

    for b in range(BRICKS):

        def brick(*offsets, b=b):
            return lookup[b * 26 + code_of(*offsets)]

        def keep(side, b=b):
            for step in range(3):
                for inner in range(3):
                    first = (step * 3 + inner) * 256
                    window[side, b * 64 : b * 64 + 64, first : first + 256] = (
                        shifted[side, inner, step : step + 8].reshape(64, 256).astype(BF16)
                    )

        for side, off in enumerate((-1, 1)):
            edge = 7 if off < 0 else 0
            for off_y in (-1, 0, 1):
                bricks = [brick(off, off_y, off_z) for off_z in (-1, 0, 1)]
                low, deep, to = ((7, 1, 0), (0, 8, 1), (0, 1, 9))[off_y + 1]
                first = edge * 64 + low * 8
                line = [
                    rows_from(pool, n, pl.ds(first, deep * 8)).reshape(deep, 8, 256)
                    for n in bricks
                ]
                for step, rows in enumerate(shift_rows(line)):
                    shifted[side, step, to : to + deep] = rows
            keep(side)
            bricks = [brick(0, off, off_z) for off_z in (-1, 0, 1)]
            for x in range(8):
                first = x * 64 + edge * 8
                line = [rows_from(pool, n, pl.ds(first, 8)).reshape(1, 8, 256) for n in bricks]
                for step, rows in enumerate(shift_rows(line)):
                    shifted[2 + side, step, 1 + x : 2 + x] = rows
            keep(2 + side)
            face = rows_from(pool, brick(0, 0, off), pl.ds(edge, 64, stride=8)).reshape(8, 8, 256)
            y = lax.broadcasted_iota(I32, face.shape, 1)
            shifted[4 + side, 0, 1:9] = jnp.where(y == 0, 0.0, pltpu.roll(face, 1, 1))
            shifted[4 + side, 1, 1:9] = face
            shifted[4 + side, 2, 1:9] = jnp.where(y == 7, 0.0, pltpu.roll(face, 7, 1))
            keep(4 + side)

    for side in range(2):
        tap = 2 * side
        added = jnp.dot(window[side], conv_weight[tap], preferred_element_type=F32)
        for b in range(BRICKS):
            first = b * 512 + 448 * side
            total[first : first + 64] += added[b * 64 : b * 64 + 64]
        added = jnp.zeros((256, 128), F32)
        for x in range(3):
            added += jnp.dot(
                window[2 + side, :, x * 768 : x * 768 + 768],
                conv_weight[x, tap * 768 : tap * 768 + 768],
                preferred_element_type=F32,
            )
        for r in range(BRICKS * 8):
            first = r * 64 + 56 * side
            total[first : first + 8] += added[r * 8 : r * 8 + 8]
        added = jnp.zeros((256, 128), F32)
        for x in range(3):
            for y in range(3):
                added += jnp.dot(
                    window[4 + side, :, (x * 3 + y) * 256 : (x * 3 + y) * 256 + 256],
                    conv_weight[x, (y * 3 + tap) * 256 : (y * 3 + tap) * 256 + 256],
                    preferred_element_type=F32,
                )
        at = pl.ds(7 * side, BRICKS * 64, stride=8)
        total[at] = total[at] + added
    out[...] = jnp.maximum(total[...], 0.0).astype(BF16).reshape(BRICKS, 512, 128)


def convolve_near(lookup, own, up_weight, pair_weight, conv_weight):
    return pl.pallas_call(
        near_kernel,
        out_shape=jax.ShapeDtypeStruct((BRICKS, 512, 128), F32),
        in_specs=[SMEM] + [VMEM] * 4,
        out_specs=VMEM,
        scratch_shapes=[
            pltpu.VMEM((BRICKS + 1, 2, 512, 128), F32),
            [pltpu.VMEM((3, 10, 10, 8, 256), F32)] * 2,
            [pltpu.VMEM((640, 9 * 256), BF16)] * 2,
        ],
        compiler_params=pltpu.CompilerParams(vmem_limit_bytes=32 * 2**20),
        cost_estimate=pl.CostEstimate(
            flops=10**10, bytes_accessed=4 * 10**7, transcendentals=0
        ),
    )(lookup, own, up_weight, pair_weight, conv_weight)


def convolve_far(lookup, before, after, near, up_weight, conv_weight):
    return pl.pallas_call(
        far_kernel,
        out_shape=jax.ShapeDtypeStruct((BRICKS, 512, 128), BF16),
        in_specs=[SMEM] + [VMEM] * 5,
        out_specs=VMEM,
        scratch_shapes=[
            pltpu.VMEM((2 * BRICKS + 1, 2, 512, 128), F32),
            pltpu.VMEM((6, 3, 10, 8, 256), F32),
            pltpu.VMEM((6, BRICKS * 64, 9 * 256), BF16),
            pltpu.VMEM((BRICKS * 512, 128), F32),
        ],
        compiler_params=pltpu.CompilerParams(vmem_limit_bytes=32 * 2**20),
    )(lookup, before, after, near, up_weight, conv_weight)


def per_device(parents, parent_dest, skip, skip_dest, neighbours, up_weight, conv_weight):
    row, inner = lax.axis_index("gx"), lax.axis_index("gy")
    devices = LINES * COLUMNS
    place = jnp.stack([inner // COLUMNS, inner % COLUMNS, row * devices * BRICKS])
    first = first_pack(parent_dest, skip_dest, place, parents, skip)
    came = [first[0]]
    for j in range(1, COLUMNS):
        steps = [(i, i // COLUMNS * COLUMNS + column_at(i % COLUMNS, j)) for i in range(devices)]
        came.append(lax.ppermute(first[j], "gy", steps))
    messages = second_pack(place, came)
    arrived = [messages[0]]
    for k in range(1, LINES):
        steps = [(i, (i + HOPS[k] * COLUMNS) % devices) for i in range(devices)]
        arrived.append(lax.ppermute(messages[k], "gy", steps))
    own, surface, flag = unpack(arrived)
    own, surface, _ = lax.while_loop(
        lambda state: state[2][0] > 0,
        lambda state: (
            *dense_route(place, parents, parent_dest, skip, skip_dest),
            jnp.zeros_like(state[2]),
        ),
        (own, surface, flag),
    )
    whole = lax.axis_size(("gx", "gy"))
    up = [(i, i + 1) for i in range(whole - 1)]
    before = lax.ppermute(surface, ("gx", "gy"), up)
    after = lax.ppermute(surface, ("gx", "gy"), [(j, i) for i, j in up])
    me = row * devices + inner
    ahead = neighbours - me * BRICKS
    here = (neighbours >= 0) & (ahead >= 0) & (ahead < BRICKS)
    near_lookup = jnp.where(here, ahead, BRICKS)
    far = jnp.where(ahead < 0, ahead + BRICKS, ahead)
    far_lookup = jnp.where((neighbours >= 0) & ~here, far, 2 * BRICKS)
    up_weight = up_weight.reshape(4, 512, 128).transpose(1, 0, 2).reshape(512, 512)
    conv_weight = conv_weight.reshape(3, 9 * 256, 128)
    pair_weight = jnp.concatenate([conv_weight[0], conv_weight[1]], axis=1)
    near = convolve_near(
        near_lookup.reshape(-1), own, up_weight, pair_weight, conv_weight
    )
    return convolve_far(far_lookup.reshape(-1), before, after, near, up_weight, conv_weight)


def solution(mesh):
    placed = (
        P(("gx", "gy"), None, None),
        P(("gx", "gy")),
        P(("gx", "gy"), None, None),
        P(("gx", "gy")),
        P(("gx", "gy"), None),
        P(),
        P(),
    )
    return jax.shard_map(
        per_device,
        mesh=mesh,
        in_specs=placed,
        out_specs=P(("gx", "gy"), None, None),
        check_vma=False,
    )
```

```python
import jax
import jax.numpy as jnp
from jax import lax
from jax.experimental import pallas as pl
from jax.experimental.pallas import tpu as pltpu
from jax.sharding import PartitionSpec as P

LINES, COLUMNS = 4, 8
SLOTS, BRICKS = 8, 4
SKIP_ROWS, PARENT_ROWS, HEAD_ROWS = 512, 128, 16
BODY = SKIP_ROWS + PARENT_ROWS
DEPTH = 2
PIECES = ((SKIP_ROWS, 0, 0), (PARENT_ROWS, SKIP_ROWS, SKIP_ROWS * DEPTH))
BF16, F32, I32 = jnp.bfloat16, jnp.float32, jnp.int32

ANY = pl.BlockSpec(memory_space=pl.ANY)
SMEM = pl.BlockSpec(memory_space=pltpu.SMEM)
VMEM = pl.BlockSpec(memory_space=pltpu.VMEM)


def rows_of(shape, values):
    row = lax.broadcasted_iota(I32, shape, 0)
    out = jnp.full(shape, -1, I32)
    for j, value in enumerate(values):
        out = jnp.where(row == j, value, out)
    return out


WAYS = ((0, 0), (0, 1), (1, 0), (3, 0), (2, 0), (2, 1), (1, 1), (3, 1))


def column_at(column, j):
    along, other = WAYS[j]
    return ((column + 2 * along) & 6) | ((column ^ other) & 1)


def first_kernel(parent_dest, skip_dest, place, parents, skip, *refs):
    outs = refs[:COLUMNS]
    slot_of, sems = refs[COLUMNS:]
    for q in range(2 * COLUMNS + 1):
        slot_of[q] = 0
    table = []
    for kind, dest in enumerate((skip_dest, parent_dest)):
        for s in range(SLOTS):
            d = dest[s]
            local = jnp.where(d >= 0, d - place[2], -1)
            table.append(local)
            column = (local >> 2) & 7
            slot_of[jnp.where(d >= 0, kind * COLUMNS + column, 2 * COLUMNS)] = s
    copies = []
    for j in range(COLUMNS):
        q = column_at(place[1], j)
        s, p = slot_of[q], slot_of[COLUMNS + q]
        copies.append(pltpu.make_async_copy(skip.at[s], outs[j].at[0:512], sems.at[j, 0]))
        for half in range(2):
            copies.append(
                pltpu.make_async_copy(
                    parents.at[p, :, 128 * half : 128 * half + 128],
                    outs[j].at[512 + 64 * half : 576 + 64 * half],
                    sems.at[j, 1 + half],
                )
            )
    for copy in copies:
        copy.start()
    head = rows_of((HEAD_ROWS, 128), table).astype(F32).astype(BF16)
    for j in range(COLUMNS):
        outs[j][BODY : BODY + HEAD_ROWS] = head
    for copy in copies:
        copy.wait()


def first_pack(parent_dest, skip_dest, place, parents, skip):
    return pl.pallas_call(
        first_kernel,
        out_shape=[jax.ShapeDtypeStruct((BODY + HEAD_ROWS, 128), BF16)] * COLUMNS,
        in_specs=[SMEM, SMEM, SMEM, ANY, ANY],
        out_specs=[VMEM] * COLUMNS,
        scratch_shapes=[
            pltpu.SMEM((2 * COLUMNS + 1,), I32),
            pltpu.SemaphoreType.DMA((COLUMNS, 3)),
        ],
        compiler_params=pltpu.CompilerParams(vmem_limit_bytes=FIRST_LIMIT),
    )(parent_dest, skip_dest, place, parents, skip)


FIRST_LIMIT = 16 * 2**20


HOPS = (0, 2, 1, 3)


def second_kernel(place, *refs):
    came, outs = refs[:COLUMNS], refs[COLUMNS : COLUMNS + LINES]
    found, table, counts, landing, sem = refs[COLUMNS + LINES :]
    line, column = place[0], place[1]
    over = jnp.zeros((1, 128), I32)
    totals = [jnp.zeros((1, 128), I32)] * 2
    row = lax.broadcasted_iota(I32, (SLOTS, 128), 0)
    lane = lax.broadcasted_iota(I32, (SLOTS, 128), 1)
    picks = jnp.full((SLOTS, 128), -1, I32)
    for m in range(COLUMNS):
        every = came[m][BODY : BODY + HEAD_ROWS].astype(F32).astype(I32)
        for kind in range(2):
            dest = every[kind * SLOTS : kind * SLOTS + SLOTS]
            live = dest >= 0
            owner = dest >> 2
            its_column = owner & 7
            mine = jnp.where(live & (its_column == column), dest, -1)
            picks = jnp.where(
                (row == m) & (lane == kind), jnp.max(mine, axis=0, keepdims=True), picks
            )
            to_column = jnp.where(live & (its_column == lane), 1, 0)
            over = over | jnp.where(jnp.sum(to_column, axis=0, keepdims=True) > 1, 1, 0)
            to_owner = jnp.where(live & (owner == lane), 1, 0)
            totals[kind] = totals[kind] + jnp.sum(to_owner, axis=0, keepdims=True)
    found[...] = picks
    copy = pltpu.make_async_copy(found, table, sem)
    copy.start()
    for j in range(2 * LINES + 1):
        counts[j] = 0
    for j in range(2 * LINES * DEPTH + 1):
        landing[j] = -1
    for kind in range(2):
        over = over | jnp.where(totals[kind] > DEPTH, 1, 0)
    flag = jnp.max(over.astype(F32), axis=1, keepdims=True).astype(I32)
    copy.wait()
    for m in range(COLUMNS):
        for kind, (rows, first, height) in enumerate(PIECES):
            dest = table[m, kind]
            live = dest >= 0
            ahead = ((dest >> 5) - line) & 3
            count_at = jnp.where(live, kind * LINES + ahead, 2 * LINES)
            rank = counts[count_at]
            counts[count_at] = rank + 1
            fits = live & (rank < DEPTH)
            spot = (kind * LINES + ahead) * DEPTH + rank
            landing[jnp.where(fits, spot, 2 * LINES * DEPTH)] = dest & 3
            at = pl.multiple_of(height + jnp.where(fits, rank, 0) * rows, 128)
            for k in range(LINES):

                @pl.when(fits & (ahead == HOPS[k]))
                def _(m=m, k=k, rows=rows, first=first, at=at):
                    outs[k][pl.ds(at, rows)] = came[m][first : first + rows]

    for k in range(LINES):
        spots = [
            landing[(kind * LINES + HOPS[k]) * DEPTH + r]
            for kind in range(2) for r in range(DEPTH)
        ]
        outs[k][BODY * DEPTH : BODY * DEPTH + HEAD_ROWS] = (
            rows_of((HEAD_ROWS, 128), spots + [flag]).astype(F32).astype(BF16)
        )


def second_pack(place, came):
    message = jax.ShapeDtypeStruct((BODY * DEPTH + HEAD_ROWS, 128), BF16)
    return pl.pallas_call(
        second_kernel,
        out_shape=[message] * LINES,
        in_specs=[SMEM] + [VMEM] * COLUMNS,
        out_specs=[VMEM] * LINES,
        scratch_shapes=[
            pltpu.VMEM((COLUMNS, 128), I32),
            pltpu.SMEM((COLUMNS, 128), I32),
            pltpu.SMEM((2 * LINES + 1,), I32),
            pltpu.SMEM((2 * LINES * DEPTH + 1,), I32),
            pltpu.SemaphoreType.DMA,
        ],
        compiler_params=pltpu.CompilerParams(vmem_limit_bytes=16 * 2**20),
    )(place, *came)


SURFACE = 352


def keep_surface(own, surface, plain):
    for b in range(BRICKS):
        plain[...] = own[b, 0:SKIP_ROWS].astype(F32)
        surface[b, 0:64] = own[b, 0:64]
        surface[b, 64:128] = own[b, 448:512]
        for side in range(2):
            lines = [
                plain[x * 64 + 56 * side : x * 64 + 56 * side + 8] for x in range(1, 7)
            ]
            surface[b, 128 + 48 * side : 176 + 48 * side] = jnp.concatenate(lines).astype(BF16)
            surface[b, 224 + 64 * side : 288 + 64 * side] = plain[
                pl.ds(7 * side, 64, stride=8)
            ].astype(BF16)
        surface[b, SURFACE : SURFACE + PARENT_ROWS] = own[b, SKIP_ROWS:BODY]


def unpack_kernel(*refs):
    came = refs[:LINES]
    own, surface, flag_out, plain = refs[LINES:]
    table = []
    for k in range(LINES):
        header = came[k][BODY * DEPTH : BODY * DEPTH + HEAD_ROWS].astype(F32).astype(I32)
        table.append([header[j, 0] for j in range(2 * DEPTH + 1)])
    flag = table[0][2 * DEPTH]
    for k in range(1, LINES):
        flag = flag | table[k][2 * DEPTH]
    flag_out[0] = flag
    for k in range(LINES):
        for kind, (rows, first, height) in enumerate(PIECES):
            for r in range(DEPTH):
                brick = table[k][kind * DEPTH + r]

                @pl.when(brick >= 0)
                def _(k=k, rows=rows, first=first, at=height + r * rows, brick=brick):
                    own[brick, first : first + rows] = came[k][at : at + rows]

    keep_surface(own, surface, plain)


def unpack(messages):
    return pl.pallas_call(
        unpack_kernel,
        out_shape=[
            jax.ShapeDtypeStruct((BRICKS, BODY, 128), BF16),
            jax.ShapeDtypeStruct((BRICKS, SURFACE + PARENT_ROWS, 128), BF16),
            jax.ShapeDtypeStruct((1,), I32),
        ],
        in_specs=[VMEM] * LINES,
        out_specs=[VMEM, VMEM, SMEM],
        scratch_shapes=[
            pltpu.VMEM((SKIP_ROWS, 128), F32),
        ],
        compiler_params=pltpu.CompilerParams(vmem_limit_bytes=16 * 2**20),
    )(*messages)


def dense_pack_kernel(parent_dest, skip_dest, place, parents, skip, out, head, sems, sem):
    table = []
    copies = []
    for kind, dest in enumerate((skip_dest, parent_dest)):
        for s in range(SLOTS):
            local = jnp.where(dest[s] >= 0, dest[s] - place[2], -1)
            table.append(local)
            owner = lax.div(jnp.maximum(local, 0), BRICKS)
            if kind == 0:
                pieces = [(skip.at[s], out.at[owner, 0:512])]
            else:
                pieces = [
                    (
                        parents.at[s, :, 128 * half : 128 * half + 128],
                        out.at[owner, 512 + 64 * half : 576 + 64 * half],
                    )
                    for half in range(2)
                ]
            for j, (source, target) in enumerate(pieces):
                copies.append(
                    (local, pltpu.make_async_copy(source, target, sems.at[s, kind + j]))
                )
    head[...] = rows_of((HEAD_ROWS, 128), table).astype(F32).astype(BF16)
    for live, copy in copies:
        pl.when(live >= 0)(copy.start)
    for owner in range(LINES * COLUMNS):
        copy = pltpu.make_async_copy(head, out.at[owner, BODY : BODY + HEAD_ROWS], sem)
        copy.start()
        copy.wait()
    for live, copy in copies:
        pl.when(live >= 0)(copy.wait)


def dense_unpack_kernel(place, came, own, surface, plain, heads, found, table, sems, sem):
    devices = LINES * COLUMNS
    copy = pltpu.make_async_copy(came.at[:, BODY : BODY + HEAD_ROWS], heads, sem)
    copy.start()
    copy.wait()
    me = place[0] * COLUMNS + place[1]
    picks = []
    for kind in range(2):
        dest = heads[:, kind * SLOTS : kind * SLOTS + SLOTS].astype(F32).astype(I32)
        mine = jnp.where((dest >= 0) & ((dest >> 2) == me), dest, -1)
        picks.append(jnp.max(mine, axis=1))
    lane = lax.broadcasted_iota(I32, (devices, 128), 1)
    found[...] = jnp.where(lane == 0, picks[0], picks[1])
    copy = pltpu.make_async_copy(found, table, sem)
    copy.start()
    copy.wait()
    for m in range(devices):
        for kind, (rows, first, _) in enumerate(PIECES):
            dest = table[m, kind]
            copy = pltpu.make_async_copy(
                came.at[m, first : first + rows],
                own.at[jnp.maximum(dest, 0) & 3, first : first + rows],
                sems.at[kind],
            )

            @pl.when(dest >= 0)
            def _(copy=copy):
                copy.start()
                copy.wait()

    keep_surface(own, surface, plain)


def dense_route(place, parents, parent_dest, skip, skip_dest):
    devices = LINES * COLUMNS
    limit = pltpu.CompilerParams(vmem_limit_bytes=16 * 2**20)
    rows = pl.pallas_call(
        dense_pack_kernel,
        out_shape=jax.ShapeDtypeStruct((devices, BODY + HEAD_ROWS, 128), BF16),
        in_specs=[SMEM, SMEM, SMEM, ANY, ANY],
        out_specs=ANY,
        scratch_shapes=[
            pltpu.VMEM((HEAD_ROWS, 128), BF16),
            pltpu.SemaphoreType.DMA((SLOTS, 3)),
            pltpu.SemaphoreType.DMA,
        ],
        compiler_params=limit,
    )(parent_dest, skip_dest, place, parents, skip)
    came = lax.all_to_all(rows, "gy", 0, 0, tiled=True)
    return pl.pallas_call(
        dense_unpack_kernel,
        out_shape=[
            jax.ShapeDtypeStruct((BRICKS, BODY, 128), BF16),
            jax.ShapeDtypeStruct((BRICKS, SURFACE + PARENT_ROWS, 128), BF16),
        ],
        in_specs=[SMEM, ANY],
        out_specs=[VMEM, VMEM],
        scratch_shapes=[
            pltpu.VMEM((SKIP_ROWS, 128), F32),
            pltpu.VMEM((devices, HEAD_ROWS, 128), BF16),
            pltpu.VMEM((devices, 128), I32),
            pltpu.SMEM((devices, 128), I32),
            pltpu.SemaphoreType.DMA((2,)),
            pltpu.SemaphoreType.DMA,
        ],
        compiler_params=limit,
    )(place, came)


def fill_pool(pool, groups, up_weight, parents_at):
    row = lax.broadcasted_iota(I32, (256, 64), 0)
    column = lax.broadcasted_iota(I32, (256, 64), 1)
    in_brick = row & 127
    takes = (in_brick >> 3) * 4 + ((in_brick & 7) >> 1) == column
    spread = jnp.where(takes & ((row & 1) == (row >> 7)), 1.0, 0.0).astype(BF16)
    for group, bricks in enumerate(groups):
        spaced = []
        for b in range(BRICKS):
            into = pool.at[group * BRICKS + b, 1]
            if parents_at == SKIP_ROWS:
                into[...] = bricks[b, 0:SKIP_ROWS].astype(F32)
            else:
                into[0:64] = bricks[b, 0:64].astype(F32)
                into[448:512] = bricks[b, 64:128].astype(F32)
                for side in range(2):
                    lines = bricks[b, 128 + 48 * side : 176 + 48 * side].astype(F32)
                    for x in range(1, 7):
                        first = x * 64 + 56 * side
                        into[first : first + 8] = lines[x * 8 - 8 : x * 8]
                    pool[group * BRICKS + b, 1, pl.ds(7 * side, 64, stride=8)] = bricks[
                        b, 224 + 64 * side : 288 + 64 * side
                    ].astype(F32)
            halves = [
                jnp.dot(
                    spread,
                    bricks[b, parents_at + 64 * h : parents_at + 64 * h + 64],
                    preferred_element_type=F32,
                ).astype(BF16)
                for h in range(2)
            ]
            spaced.append(
                jnp.concatenate(
                    [halves[0][:128], halves[1][:128], halves[0][128:], halves[1][128:]], axis=1
                )
            )
        spaced = jnp.concatenate(spaced, axis=0)
        every = jnp.dot(spaced, up_weight[...], preferred_element_type=F32)
        every = every.astype(BF16).astype(F32)
        for ab in range(4):
            made = every[:, ab * 128 : ab * 128 + 128]
            for b in range(BRICKS):
                for i in range(4):
                    for j in range(4):
                        first = (2 * i + ab // 2) * 64 + (2 * j + ab % 2) * 8
                        came = b * 128 + i * 32 + j * 8
                        pool[group * BRICKS + b, 0, first : first + 8] = made[came : came + 8]
    pool[len(groups) * BRICKS] = jnp.zeros((2, 512, 128), F32)


def rows_from(pool, brick, rows):
    return jnp.concatenate([pool[brick, 0, rows], pool[brick, 1, rows]], axis=1)


def shift_rows(line):
    z = lax.broadcasted_iota(I32, line[1].shape, 1)
    return (
        pltpu.roll(jnp.where(z == 7, line[0], line[1]), 1, 1),
        line[1],
        pltpu.roll(jnp.where(z == 0, line[2], line[1]), 7, 1),
    )


def code_of(off_x, off_y, off_z):
    code = (off_x + 1) * 9 + (off_y + 1) * 3 + off_z + 1
    return code - (code > 13)


def near_kernel(
    lookup, own, up_weight, pair_weight, side_weight, conv_weight, out,
    pool, shifted_pair, window_pair, deeper_pair
):
    fill_pool(pool, (own,), up_weight, SKIP_ROWS)
    spans = {-1: (7, 8, 0), 0: (0, 8, 1), 1: (0, 1, 9)}

    for b in range(BRICKS):
        shifted, window, deeper = shifted_pair[b % 2], window_pair[b % 2], deeper_pair[b % 2]
        for off_x in (-1, 0, 1):
            for off_y in (-1, 0, 1):
                low_x, high_x, to_x = spans[off_x]
                low_y, high_y, to_y = spans[off_y]
                deep = high_y - low_y
                bricks = [
                    b if off_x == off_y == off_z == 0 else lookup[b * 26 + code_of(off_x, off_y, off_z)]
                    for off_z in (-1, 0, 1)
                ]
                for x in range(low_x, high_x):
                    first = x * 64 + low_y * 8
                    line = [
                        rows_from(pool, brick, pl.ds(first, deep * 8)).reshape(deep, 8, 256)
                        for brick in bricks
                    ]
                    for step, rows in enumerate(shift_rows(line)):
                        shifted[step, to_x + x - low_x, to_y : to_y + deep] = rows
        for step_y in range(3):
            for step_z in range(3):
                first = (step_y * 3 + step_z) * 256
                window[:, first : first + 256] = (
                    shifted[step_z, :, step_y : step_y + 8].reshape(640, 256).astype(BF16)
                )
        for step_z in range(3):
            deeper[:, step_z * 256 : step_z * 256 + 256] = (
                shifted[step_z, 2:10, 0:9].reshape(576, 256).astype(BF16)
            )
        pair = jnp.dot(window[0:576], pair_weight[...], preferred_element_type=F32)
        side = jnp.dot(deeper[...], side_weight[...], preferred_element_type=F32)
        side = side.reshape(8, 9, 8, 256)
        side = (side[:, 0:8, :, 0:128] + side[:, 1:9, :, 128:256]).reshape(512, 128)
        last = jnp.dot(
            window[128:640, 1536:2304], conv_weight[2, 1536:2304], preferred_element_type=F32
        )
        out[b] = pair[0:512, 0:128] + pair[64:576, 128:256] + side + last


def far_kernel(
    lookup, before, after, near, up_weight, conv_weight, out, pool, shifted, window, total
):
    fill_pool(pool, (before, after), up_weight, SURFACE)
    total[...] = near[...].reshape(BRICKS * 512, 128)
    shifted[...] = jnp.zeros(shifted.shape, F32)

    def brick(b, *offsets):
        return lookup[b * 26 + code_of(*offsets)]

    def keep(face, b):
        for step in range(3):
            for inner in range(3):
                first = (step * 3 + inner) * 256
                window[face, b * 64 : b * 64 + 64, first : first + 256] = (
                    shifted[face, inner, step : step + 8].reshape(64, 256).astype(BF16)
                )

    for side, off in enumerate((-1, 1)):
        edge, tap = (7 if off < 0 else 0), 2 * side
        for b in range(BRICKS):
            for off_y in (-1, 0, 1):
                low, deep, to = ((7, 1, 0), (0, 8, 1), (0, 1, 9))[off_y + 1]
                first = edge * 64 + low * 8
                line = [
                    rows_from(pool, brick(b, off, off_y, off_z), pl.ds(first, deep * 8)).reshape(
                        deep, 8, 256
                    )
                    for off_z in (-1, 0, 1)
                ]
                for step, rows in enumerate(shift_rows(line)):
                    shifted[side, step, to : to + deep] = rows
            keep(side, b)
        added = jnp.dot(window[side], conv_weight[tap], preferred_element_type=F32)
        for b in range(BRICKS):
            first = b * 512 + 448 * side
            total[first : first + 64] += added[b * 64 : b * 64 + 64]
        for b in range(BRICKS):
            bricks = [brick(b, 0, off, off_z) for off_z in (-1, 0, 1)]
            for x in range(8):
                first = x * 64 + edge * 8
                line = [rows_from(pool, n, pl.ds(first, 8)).reshape(1, 8, 256) for n in bricks]
                for step, rows in enumerate(shift_rows(line)):
                    shifted[2 + side, step, 1 + x : 2 + x] = rows
            keep(2 + side, b)
        added = jnp.zeros((256, 128), F32)
        for x in range(3):
            added += jnp.dot(
                window[2 + side, :, x * 768 : x * 768 + 768],
                conv_weight[x, tap * 768 : tap * 768 + 768],
                preferred_element_type=F32,
            )
        for r in range(BRICKS * 8):
            first = r * 64 + 56 * side
            total[first : first + 8] += added[r * 8 : r * 8 + 8]
        for b in range(BRICKS):
            face = rows_from(pool, brick(b, 0, 0, off), pl.ds(edge, 64, stride=8)).reshape(8, 8, 256)
            y = lax.broadcasted_iota(I32, face.shape, 1)
            shifted[4 + side, 0, 1:9] = jnp.where(y == 0, 0.0, pltpu.roll(face, 1, 1))
            shifted[4 + side, 1, 1:9] = face
            shifted[4 + side, 2, 1:9] = jnp.where(y == 7, 0.0, pltpu.roll(face, 7, 1))
            keep(4 + side, b)
        added = jnp.zeros((256, 128), F32)
        for x in range(3):
            for y in range(3):
                added += jnp.dot(
                    window[4 + side, :, (x * 3 + y) * 256 : (x * 3 + y) * 256 + 256],
                    conv_weight[x, (y * 3 + tap) * 256 : (y * 3 + tap) * 256 + 256],
                    preferred_element_type=F32,
                )
        at = pl.ds(7 * side, BRICKS * 64, stride=8)
        total[at] = total[at] + added
    out[...] = jnp.maximum(total[...], 0.0).astype(BF16).reshape(BRICKS, 512, 128)


def convolve_near(lookup, own, up_weight, pair_weight, side_weight, conv_weight):
    return pl.pallas_call(
        near_kernel,
        out_shape=jax.ShapeDtypeStruct((BRICKS, 512, 128), F32),
        in_specs=[SMEM] + [VMEM] * 5,
        out_specs=VMEM,
        scratch_shapes=[
            pltpu.VMEM((BRICKS + 1, 2, 512, 128), F32),
            [pltpu.VMEM((3, 10, 10, 8, 256), F32)] * 2,
            [pltpu.VMEM((640, 9 * 256), BF16)] * 2,
            [pltpu.VMEM((576, 3 * 256), BF16)] * 2,
        ],
        compiler_params=pltpu.CompilerParams(vmem_limit_bytes=32 * 2**20),
        cost_estimate=pl.CostEstimate(
            flops=10**10, bytes_accessed=4 * 10**7, transcendentals=0
        ),
    )(lookup, own, up_weight, pair_weight, side_weight, conv_weight)


def convolve_far(lookup, before, after, near, up_weight, conv_weight):
    return pl.pallas_call(
        far_kernel,
        out_shape=jax.ShapeDtypeStruct((BRICKS, 512, 128), BF16),
        in_specs=[SMEM] + [VMEM] * 5,
        out_specs=VMEM,
        scratch_shapes=[
            pltpu.VMEM((2 * BRICKS + 1, 2, 512, 128), F32),
            pltpu.VMEM((6, 3, 10, 8, 256), F32),
            pltpu.VMEM((6, BRICKS * 64, 9 * 256), BF16),
            pltpu.VMEM((BRICKS * 512, 128), F32),
        ],
        compiler_params=pltpu.CompilerParams(vmem_limit_bytes=32 * 2**20),
    )(lookup, before, after, near, up_weight, conv_weight)


def per_device(parents, parent_dest, skip, skip_dest, neighbours, up_weight, conv_weight):
    row, inner = lax.axis_index("gx"), lax.axis_index("gy")
    devices = LINES * COLUMNS
    place = jnp.stack([inner // COLUMNS, inner % COLUMNS, row * devices * BRICKS])
    first = first_pack(parent_dest, skip_dest, place, parents, skip)
    came = [first[0]]
    for j in range(1, COLUMNS):
        steps = [(i, i // COLUMNS * COLUMNS + column_at(i % COLUMNS, j)) for i in range(devices)]
        came.append(lax.ppermute(first[j], "gy", steps))
    messages = second_pack(place, came)
    arrived = [messages[0]]
    for k in range(1, LINES):
        steps = [(i, (i + HOPS[k] * COLUMNS) % devices) for i in range(devices)]
        arrived.append(lax.ppermute(messages[k], "gy", steps))
    own, surface, flag = unpack(arrived)
    own, surface, _ = lax.while_loop(
        lambda state: state[2][0] > 0,
        lambda state: (
            *dense_route(place, parents, parent_dest, skip, skip_dest),
            jnp.zeros_like(state[2]),
        ),
        (own, surface, flag),
    )
    whole = lax.axis_size(("gx", "gy"))
    up = [(i, i + 1) for i in range(whole - 1)]
    before = lax.ppermute(surface, ("gx", "gy"), up)
    after = lax.ppermute(surface, ("gx", "gy"), [(j, i) for i, j in up])
    me = row * devices + inner
    ahead = neighbours - me * BRICKS
    here = (neighbours >= 0) & (ahead >= 0) & (ahead < BRICKS)
    near_lookup = jnp.where(here, ahead, BRICKS)
    far = jnp.where(ahead < 0, ahead + BRICKS, ahead)
    far_lookup = jnp.where((neighbours >= 0) & ~here, far, 2 * BRICKS)
    up_weight = up_weight.reshape(4, 512, 128).transpose(1, 0, 2).reshape(512, 512)
    conv_weight = conv_weight.reshape(3, 9 * 256, 128)
    pair_weight = jnp.concatenate([conv_weight[0], conv_weight[1]], axis=1)
    side_weight = jnp.concatenate([conv_weight[2, 0:768], conv_weight[2, 768:1536]], axis=1)
    near = convolve_near(
        near_lookup.reshape(-1), own, up_weight, pair_weight, side_weight, conv_weight
    )
    return convolve_far(far_lookup.reshape(-1), before, after, near, up_weight, conv_weight)


def solution(mesh):
    placed = (
        P(("gx", "gy"), None, None),
        P(("gx", "gy")),
        P(("gx", "gy"), None, None),
        P(("gx", "gy")),
        P(("gx", "gy"), None),
        P(),
        P(),
    )
    return jax.shard_map(
        per_device,
        mesh=mesh,
        in_specs=placed,
        out_specs=P(("gx", "gy"), None, None),
        check_vma=False,
    )
```

```python
import jax
import jax.numpy as jnp
from jax import lax
from jax.experimental import pallas as pl
from jax.experimental.pallas import tpu as pltpu
from jax.sharding import PartitionSpec as P

LINES, COLUMNS = 4, 8
SLOTS, BRICKS = 8, 4
SKIP_ROWS, PARENT_ROWS, HEAD_ROWS = 512, 128, 16
BODY = SKIP_ROWS + PARENT_ROWS
DEPTH = 2
PIECES = ((SKIP_ROWS, 0, 0), (PARENT_ROWS, SKIP_ROWS, SKIP_ROWS * DEPTH))
BF16, F32, I32 = jnp.bfloat16, jnp.float32, jnp.int32

ANY = pl.BlockSpec(memory_space=pl.ANY)
SMEM = pl.BlockSpec(memory_space=pltpu.SMEM)
VMEM = pl.BlockSpec(memory_space=pltpu.VMEM)


def rows_of(shape, values):
    row = lax.broadcasted_iota(I32, shape, 0)
    out = jnp.full(shape, -1, I32)
    for j, value in enumerate(values):
        out = jnp.where(row == j, value, out)
    return out


WAYS = ((0, 0), (0, 1), (1, 0), (3, 0), (2, 0), (2, 1), (1, 1), (3, 1))


def column_at(column, j):
    along, other = WAYS[j]
    return ((column + 2 * along) & 6) | ((column ^ other) & 1)


def first_kernel(parent_dest, skip_dest, place, parents, skip, *refs):
    outs = refs[:COLUMNS]
    slot_of, sems = refs[COLUMNS:]
    for q in range(2 * COLUMNS + 1):
        slot_of[q] = 0
    table = []
    for kind, dest in enumerate((skip_dest, parent_dest)):
        for s in range(SLOTS):
            d = dest[s]
            local = jnp.where(d >= 0, d - place[2], -1)
            table.append(local)
            column = (local >> 2) & 7
            slot_of[jnp.where(d >= 0, kind * COLUMNS + column, 2 * COLUMNS)] = s
    copies = []
    for j in range(COLUMNS):
        q = column_at(place[1], j)
        s, p = slot_of[q], slot_of[COLUMNS + q]
        copies.append(pltpu.make_async_copy(skip.at[s], outs[j].at[0:512], sems.at[j, 0]))
        for half in range(2):
            copies.append(
                pltpu.make_async_copy(
                    parents.at[p, :, 128 * half : 128 * half + 128],
                    outs[j].at[512 + 64 * half : 576 + 64 * half],
                    sems.at[j, 1 + half],
                )
            )
    for copy in copies:
        copy.start()
    head = rows_of((HEAD_ROWS, 128), table).astype(F32).astype(BF16)
    for j in range(COLUMNS):
        outs[j][BODY : BODY + HEAD_ROWS] = head
    for copy in copies:
        copy.wait()


def first_pack(parent_dest, skip_dest, place, parents, skip):
    return pl.pallas_call(
        first_kernel,
        out_shape=[jax.ShapeDtypeStruct((BODY + HEAD_ROWS, 128), BF16)] * COLUMNS,
        in_specs=[SMEM, SMEM, SMEM, ANY, ANY],
        out_specs=[VMEM] * COLUMNS,
        scratch_shapes=[
            pltpu.SMEM((2 * COLUMNS + 1,), I32),
            pltpu.SemaphoreType.DMA((COLUMNS, 3)),
        ],
        compiler_params=pltpu.CompilerParams(vmem_limit_bytes=FIRST_LIMIT),
    )(parent_dest, skip_dest, place, parents, skip)


FIRST_LIMIT = 16 * 2**20


HOPS = (0, 2, 1, 3)


def second_kernel(place, *refs):
    came, outs = refs[:COLUMNS], refs[COLUMNS : COLUMNS + LINES]
    found, table, counts, landing, sem = refs[COLUMNS + LINES :]
    line, column = place[0], place[1]
    over = jnp.zeros((1, 128), I32)
    totals = [jnp.zeros((1, 128), I32)] * 2
    row = lax.broadcasted_iota(I32, (SLOTS, 128), 0)
    lane = lax.broadcasted_iota(I32, (SLOTS, 128), 1)
    picks = jnp.full((SLOTS, 128), -1, I32)
    for m in range(COLUMNS):
        every = came[m][BODY : BODY + HEAD_ROWS].astype(F32).astype(I32)
        for kind in range(2):
            dest = every[kind * SLOTS : kind * SLOTS + SLOTS]
            live = dest >= 0
            owner = dest >> 2
            its_column = owner & 7
            mine = jnp.where(live & (its_column == column), dest, -1)
            picks = jnp.where(
                (row == m) & (lane == kind), jnp.max(mine, axis=0, keepdims=True), picks
            )
            to_column = jnp.where(live & (its_column == lane), 1, 0)
            over = over | jnp.where(jnp.sum(to_column, axis=0, keepdims=True) > 1, 1, 0)
            to_owner = jnp.where(live & (owner == lane), 1, 0)
            totals[kind] = totals[kind] + jnp.sum(to_owner, axis=0, keepdims=True)
    found[...] = picks
    copy = pltpu.make_async_copy(found, table, sem)
    copy.start()
    for j in range(2 * LINES + 1):
        counts[j] = 0
    for j in range(2 * LINES * DEPTH + 1):
        landing[j] = -1
    for kind in range(2):
        over = over | jnp.where(totals[kind] > DEPTH, 1, 0)
    flag = jnp.max(over.astype(F32), axis=1, keepdims=True).astype(I32)
    copy.wait()
    for m in range(COLUMNS):
        for kind, (rows, first, height) in enumerate(PIECES):
            dest = table[m, kind]
            live = dest >= 0
            ahead = ((dest >> 5) - line) & 3
            count_at = jnp.where(live, kind * LINES + ahead, 2 * LINES)
            rank = counts[count_at]
            counts[count_at] = rank + 1
            fits = live & (rank < DEPTH)
            spot = (kind * LINES + ahead) * DEPTH + rank
            landing[jnp.where(fits, spot, 2 * LINES * DEPTH)] = dest & 3
            at = pl.multiple_of(height + jnp.where(fits, rank, 0) * rows, 128)
            for k in range(LINES):

                @pl.when(fits & (ahead == HOPS[k]))
                def _(m=m, k=k, rows=rows, first=first, at=at):
                    outs[k][pl.ds(at, rows)] = came[m][first : first + rows]

    for k in range(LINES):
        spots = [
            landing[(kind * LINES + HOPS[k]) * DEPTH + r]
            for kind in range(2) for r in range(DEPTH)
        ]
        outs[k][BODY * DEPTH : BODY * DEPTH + HEAD_ROWS] = (
            rows_of((HEAD_ROWS, 128), spots + [flag]).astype(F32).astype(BF16)
        )


def second_pack(place, came):
    message = jax.ShapeDtypeStruct((BODY * DEPTH + HEAD_ROWS, 128), BF16)
    return pl.pallas_call(
        second_kernel,
        out_shape=[message] * LINES,
        in_specs=[SMEM] + [VMEM] * COLUMNS,
        out_specs=[VMEM] * LINES,
        scratch_shapes=[
            pltpu.VMEM((COLUMNS, 128), I32),
            pltpu.SMEM((COLUMNS, 128), I32),
            pltpu.SMEM((2 * LINES + 1,), I32),
            pltpu.SMEM((2 * LINES * DEPTH + 1,), I32),
            pltpu.SemaphoreType.DMA,
        ],
        compiler_params=pltpu.CompilerParams(vmem_limit_bytes=16 * 2**20),
    )(place, *came)


SURFACE = 352


def keep_surface(own, surface, plain):
    for b in range(BRICKS):
        plain[...] = own[b, 0:SKIP_ROWS].astype(F32)
        surface[b, 0:64] = own[b, 0:64]
        surface[b, 64:128] = own[b, 448:512]
        for side in range(2):
            lines = [
                plain[x * 64 + 56 * side : x * 64 + 56 * side + 8] for x in range(1, 7)
            ]
            surface[b, 128 + 48 * side : 176 + 48 * side] = jnp.concatenate(lines).astype(BF16)
            surface[b, 224 + 64 * side : 288 + 64 * side] = plain[
                pl.ds(7 * side, 64, stride=8)
            ].astype(BF16)
        surface[b, SURFACE : SURFACE + PARENT_ROWS] = own[b, SKIP_ROWS:BODY]


def unpack_kernel(*refs):
    came = refs[:LINES]
    own, surface, flag_out, plain = refs[LINES:]
    table = []
    for k in range(LINES):
        header = came[k][BODY * DEPTH : BODY * DEPTH + HEAD_ROWS].astype(F32).astype(I32)
        table.append([header[j, 0] for j in range(2 * DEPTH + 1)])
    flag = table[0][2 * DEPTH]
    for k in range(1, LINES):
        flag = flag | table[k][2 * DEPTH]
    flag_out[0] = flag
    for k in range(LINES):
        for kind, (rows, first, height) in enumerate(PIECES):
            for r in range(DEPTH):
                brick = table[k][kind * DEPTH + r]

                @pl.when(brick >= 0)
                def _(k=k, rows=rows, first=first, at=height + r * rows, brick=brick):
                    own[brick, first : first + rows] = came[k][at : at + rows]

    keep_surface(own, surface, plain)


def unpack(messages):
    return pl.pallas_call(
        unpack_kernel,
        out_shape=[
            jax.ShapeDtypeStruct((BRICKS, BODY, 128), BF16),
            jax.ShapeDtypeStruct((BRICKS, SURFACE + PARENT_ROWS, 128), BF16),
            jax.ShapeDtypeStruct((1,), I32),
        ],
        in_specs=[VMEM] * LINES,
        out_specs=[VMEM, VMEM, SMEM],
        scratch_shapes=[
            pltpu.VMEM((SKIP_ROWS, 128), F32),
        ],
        compiler_params=pltpu.CompilerParams(vmem_limit_bytes=16 * 2**20),
    )(*messages)


def dense_pack_kernel(parent_dest, skip_dest, place, parents, skip, out, head, sems, sem):
    table = []
    copies = []
    for kind, dest in enumerate((skip_dest, parent_dest)):
        for s in range(SLOTS):
            local = jnp.where(dest[s] >= 0, dest[s] - place[2], -1)
            table.append(local)
            owner = lax.div(jnp.maximum(local, 0), BRICKS)
            if kind == 0:
                pieces = [(skip.at[s], out.at[owner, 0:512])]
            else:
                pieces = [
                    (
                        parents.at[s, :, 128 * half : 128 * half + 128],
                        out.at[owner, 512 + 64 * half : 576 + 64 * half],
                    )
                    for half in range(2)
                ]
            for j, (source, target) in enumerate(pieces):
                copies.append(
                    (local, pltpu.make_async_copy(source, target, sems.at[s, kind + j]))
                )
    head[...] = rows_of((HEAD_ROWS, 128), table).astype(F32).astype(BF16)
    for live, copy in copies:
        pl.when(live >= 0)(copy.start)
    for owner in range(LINES * COLUMNS):
        copy = pltpu.make_async_copy(head, out.at[owner, BODY : BODY + HEAD_ROWS], sem)
        copy.start()
        copy.wait()
    for live, copy in copies:
        pl.when(live >= 0)(copy.wait)


def dense_unpack_kernel(place, came, own, surface, plain, heads, found, table, sems, sem):
    devices = LINES * COLUMNS
    copy = pltpu.make_async_copy(came.at[:, BODY : BODY + HEAD_ROWS], heads, sem)
    copy.start()
    copy.wait()
    me = place[0] * COLUMNS + place[1]
    picks = []
    for kind in range(2):
        dest = heads[:, kind * SLOTS : kind * SLOTS + SLOTS].astype(F32).astype(I32)
        mine = jnp.where((dest >= 0) & ((dest >> 2) == me), dest, -1)
        picks.append(jnp.max(mine, axis=1))
    lane = lax.broadcasted_iota(I32, (devices, 128), 1)
    found[...] = jnp.where(lane == 0, picks[0], picks[1])
    copy = pltpu.make_async_copy(found, table, sem)
    copy.start()
    copy.wait()
    for m in range(devices):
        for kind, (rows, first, _) in enumerate(PIECES):
            dest = table[m, kind]
            copy = pltpu.make_async_copy(
                came.at[m, first : first + rows],
                own.at[jnp.maximum(dest, 0) & 3, first : first + rows],
                sems.at[kind],
            )

            @pl.when(dest >= 0)
            def _(copy=copy):
                copy.start()
                copy.wait()

    keep_surface(own, surface, plain)


def dense_route(place, parents, parent_dest, skip, skip_dest):
    devices = LINES * COLUMNS
    limit = pltpu.CompilerParams(vmem_limit_bytes=16 * 2**20)
    rows = pl.pallas_call(
        dense_pack_kernel,
        out_shape=jax.ShapeDtypeStruct((devices, BODY + HEAD_ROWS, 128), BF16),
        in_specs=[SMEM, SMEM, SMEM, ANY, ANY],
        out_specs=ANY,
        scratch_shapes=[
            pltpu.VMEM((HEAD_ROWS, 128), BF16),
            pltpu.SemaphoreType.DMA((SLOTS, 3)),
            pltpu.SemaphoreType.DMA,
        ],
        compiler_params=limit,
    )(parent_dest, skip_dest, place, parents, skip)
    came = lax.all_to_all(rows, "gy", 0, 0, tiled=True)
    return pl.pallas_call(
        dense_unpack_kernel,
        out_shape=[
            jax.ShapeDtypeStruct((BRICKS, BODY, 128), BF16),
            jax.ShapeDtypeStruct((BRICKS, SURFACE + PARENT_ROWS, 128), BF16),
        ],
        in_specs=[SMEM, ANY],
        out_specs=[VMEM, VMEM],
        scratch_shapes=[
            pltpu.VMEM((SKIP_ROWS, 128), F32),
            pltpu.VMEM((devices, HEAD_ROWS, 128), BF16),
            pltpu.VMEM((devices, 128), I32),
            pltpu.SMEM((devices, 128), I32),
            pltpu.SemaphoreType.DMA((2,)),
            pltpu.SemaphoreType.DMA,
        ],
        compiler_params=limit,
    )(place, came)


def fill_pool(pool, groups, up_weight, up_all, parents_at):
    for ab in range(4):
        up_all[:, 128 * ab : 128 * ab + 128] = up_weight[ab]
    row = lax.broadcasted_iota(I32, (256, 64), 0)
    column = lax.broadcasted_iota(I32, (256, 64), 1)
    in_brick = row & 127
    takes = (in_brick >> 3) * 4 + ((in_brick & 7) >> 1) == column
    spread = jnp.where(takes & ((row & 1) == (row >> 7)), 1.0, 0.0).astype(BF16)
    for group, bricks in enumerate(groups):
        spaced = []
        for b in range(BRICKS):
            into = pool.at[group * BRICKS + b, 1]
            if parents_at == SKIP_ROWS:
                into[...] = bricks[b, 0:SKIP_ROWS].astype(F32)
            else:
                into[0:64] = bricks[b, 0:64].astype(F32)
                into[448:512] = bricks[b, 64:128].astype(F32)
                for side in range(2):
                    lines = bricks[b, 128 + 48 * side : 176 + 48 * side].astype(F32)
                    for x in range(1, 7):
                        first = x * 64 + 56 * side
                        into[first : first + 8] = lines[x * 8 - 8 : x * 8]
                    pool[group * BRICKS + b, 1, pl.ds(7 * side, 64, stride=8)] = bricks[
                        b, 224 + 64 * side : 288 + 64 * side
                    ].astype(F32)
            halves = [
                jnp.dot(
                    spread,
                    bricks[b, parents_at + 64 * h : parents_at + 64 * h + 64],
                    preferred_element_type=F32,
                ).astype(BF16)
                for h in range(2)
            ]
            spaced.append(
                jnp.concatenate(
                    [halves[0][:128], halves[1][:128], halves[0][128:], halves[1][128:]], axis=1
                )
            )
        spaced = jnp.concatenate(spaced, axis=0)
        every = jnp.dot(spaced, up_all[...], preferred_element_type=F32)
        every = every.astype(BF16).astype(F32)
        for ab in range(4):
            made = every[:, ab * 128 : ab * 128 + 128]
            for b in range(BRICKS):
                for i in range(4):
                    for j in range(4):
                        first = (2 * i + ab // 2) * 64 + (2 * j + ab % 2) * 8
                        came = b * 128 + i * 32 + j * 8
                        pool[group * BRICKS + b, 0, first : first + 8] = made[came : came + 8]
    pool[len(groups) * BRICKS] = jnp.zeros((2, 512, 128), F32)


def rows_from(pool, brick, rows):
    return jnp.concatenate([pool[brick, 0, rows], pool[brick, 1, rows]], axis=1)


def shift_rows(line):
    z = lax.broadcasted_iota(I32, line[1].shape, 1)
    return (
        pltpu.roll(jnp.where(z == 7, line[0], line[1]), 1, 1),
        line[1],
        pltpu.roll(jnp.where(z == 0, line[2], line[1]), 7, 1),
    )


def code_of(off_x, off_y, off_z):
    code = (off_x + 1) * 9 + (off_y + 1) * 3 + off_z + 1
    return code - (code > 13)


def near_kernel(
    lookup, own, up_weight, conv_weight, out,
    pool, shifted_pair, window_pair, deeper_pair, pair_weight, side_weight, up_all
):
    for half in range(2):
        columns = slice(128 * half, 128 * half + 128)
        pair_weight[:, columns] = conv_weight[half]
        side_weight[:, columns] = conv_weight[2, 768 * half : 768 * half + 768]
    fill_pool(pool, (own,), up_weight, up_all, SKIP_ROWS)
    spans = {-1: (7, 8, 0), 0: (0, 8, 1), 1: (0, 1, 9)}

    for b in range(BRICKS):
        shifted, window, deeper = shifted_pair[b % 2], window_pair[b % 2], deeper_pair[b % 2]
        for off_x in (-1, 0, 1):
            for off_y in (-1, 0, 1):
                low_x, high_x, to_x = spans[off_x]
                low_y, high_y, to_y = spans[off_y]
                deep = high_y - low_y
                bricks = [
                    b if off_x == off_y == off_z == 0 else lookup[b * 26 + code_of(off_x, off_y, off_z)]
                    for off_z in (-1, 0, 1)
                ]
                for x in range(low_x, high_x):
                    first = x * 64 + low_y * 8
                    line = [
                        rows_from(pool, brick, pl.ds(first, deep * 8)).reshape(deep, 8, 256)
                        for brick in bricks
                    ]
                    for step, rows in enumerate(shift_rows(line)):
                        shifted[step, to_x + x - low_x, to_y : to_y + deep] = rows
        for step_y in range(3):
            for step_z in range(3):
                first = (step_y * 3 + step_z) * 256
                window[:, first : first + 256] = (
                    shifted[step_z, :, step_y : step_y + 8].reshape(640, 256).astype(BF16)
                )
        for step_z in range(3):
            deeper[:, step_z * 256 : step_z * 256 + 256] = (
                shifted[step_z, 2:10, 0:9].reshape(576, 256).astype(BF16)
            )
        pair = jnp.dot(window[0:576], pair_weight[...], preferred_element_type=F32)
        side = jnp.dot(deeper[...], side_weight[...], preferred_element_type=F32)
        side = side.reshape(8, 9, 8, 256)
        side = (side[:, 0:8, :, 0:128] + side[:, 1:9, :, 128:256]).reshape(512, 128)
        last = jnp.dot(
            window[128:640, 1536:2304], conv_weight[2, 1536:2304], preferred_element_type=F32
        )
        out[b] = pair[0:512, 0:128] + pair[64:576, 128:256] + side + last


def far_kernel(
    lookup, before, after, near, up_weight, conv_weight, out, pool, shifted, window, total, up_all
):
    fill_pool(pool, (before, after), up_weight, up_all, SURFACE)
    total[...] = near[...].reshape(BRICKS * 512, 128)
    shifted[...] = jnp.zeros(shifted.shape, F32)

    def brick(b, *offsets):
        return lookup[b * 26 + code_of(*offsets)]

    def keep(face, b):
        for step in range(3):
            for inner in range(3):
                first = (step * 3 + inner) * 256
                window[face, b * 64 : b * 64 + 64, first : first + 256] = (
                    shifted[face, inner, step : step + 8].reshape(64, 256).astype(BF16)
                )

    for side, off in enumerate((-1, 1)):
        edge, tap = (7 if off < 0 else 0), 2 * side
        for b in range(BRICKS):
            for off_y in (-1, 0, 1):
                low, deep, to = ((7, 1, 0), (0, 8, 1), (0, 1, 9))[off_y + 1]
                first = edge * 64 + low * 8
                line = [
                    rows_from(pool, brick(b, off, off_y, off_z), pl.ds(first, deep * 8)).reshape(
                        deep, 8, 256
                    )
                    for off_z in (-1, 0, 1)
                ]
                for step, rows in enumerate(shift_rows(line)):
                    shifted[side, step, to : to + deep] = rows
            keep(side, b)
        added = jnp.dot(window[side], conv_weight[tap], preferred_element_type=F32)
        for b in range(BRICKS):
            first = b * 512 + 448 * side
            total[first : first + 64] += added[b * 64 : b * 64 + 64]
        for b in range(BRICKS):
            bricks = [brick(b, 0, off, off_z) for off_z in (-1, 0, 1)]
            for x in range(8):
                first = x * 64 + edge * 8
                line = [rows_from(pool, n, pl.ds(first, 8)).reshape(1, 8, 256) for n in bricks]
                for step, rows in enumerate(shift_rows(line)):
                    shifted[2 + side, step, 1 + x : 2 + x] = rows
            keep(2 + side, b)
        added = jnp.zeros((256, 128), F32)
        for x in range(3):
            added += jnp.dot(
                window[2 + side, :, x * 768 : x * 768 + 768],
                conv_weight[x, tap * 768 : tap * 768 + 768],
                preferred_element_type=F32,
            )
        for r in range(BRICKS * 8):
            first = r * 64 + 56 * side
            total[first : first + 8] += added[r * 8 : r * 8 + 8]
        for b in range(BRICKS):
            face = rows_from(pool, brick(b, 0, 0, off), pl.ds(edge, 64, stride=8)).reshape(8, 8, 256)
            y = lax.broadcasted_iota(I32, face.shape, 1)
            shifted[4 + side, 0, 1:9] = jnp.where(y == 0, 0.0, pltpu.roll(face, 1, 1))
            shifted[4 + side, 1, 1:9] = face
            shifted[4 + side, 2, 1:9] = jnp.where(y == 7, 0.0, pltpu.roll(face, 7, 1))
            keep(4 + side, b)
        added = jnp.zeros((256, 128), F32)
        for x in range(3):
            for y in range(3):
                added += jnp.dot(
                    window[4 + side, :, (x * 3 + y) * 256 : (x * 3 + y) * 256 + 256],
                    conv_weight[x, (y * 3 + tap) * 256 : (y * 3 + tap) * 256 + 256],
                    preferred_element_type=F32,
                )
        at = pl.ds(7 * side, BRICKS * 64, stride=8)
        total[at] = total[at] + added
    out[...] = jnp.maximum(total[...], 0.0).astype(BF16).reshape(BRICKS, 512, 128)


def convolve_near(lookup, own, up_weight, conv_weight):
    return pl.pallas_call(
        near_kernel,
        out_shape=jax.ShapeDtypeStruct((BRICKS, 512, 128), F32),
        in_specs=[SMEM] + [VMEM] * 3,
        out_specs=VMEM,
        scratch_shapes=[
            pltpu.VMEM((BRICKS + 1, 2, 512, 128), F32),
            [pltpu.VMEM((3, 10, 10, 8, 256), F32)] * 2,
            [pltpu.VMEM((640, 9 * 256), BF16)] * 2,
            [pltpu.VMEM((576, 3 * 256), BF16)] * 2,
            pltpu.VMEM((9 * 256, 256), BF16),
            pltpu.VMEM((3 * 256, 256), BF16),
            pltpu.VMEM((512, 512), BF16),
        ],
        compiler_params=pltpu.CompilerParams(vmem_limit_bytes=32 * 2**20),
        cost_estimate=pl.CostEstimate(
            flops=10**10, bytes_accessed=4 * 10**7, transcendentals=0
        ),
    )(lookup, own, up_weight, conv_weight)


def convolve_far(lookup, before, after, near, up_weight, conv_weight):
    return pl.pallas_call(
        far_kernel,
        out_shape=jax.ShapeDtypeStruct((BRICKS, 512, 128), BF16),
        in_specs=[SMEM] + [VMEM] * 5,
        out_specs=VMEM,
        scratch_shapes=[
            pltpu.VMEM((2 * BRICKS + 1, 2, 512, 128), F32),
            pltpu.VMEM((6, 3, 10, 8, 256), F32),
            pltpu.VMEM((6, BRICKS * 64, 9 * 256), BF16),
            pltpu.VMEM((BRICKS * 512, 128), F32),
            pltpu.VMEM((512, 512), BF16),
        ],
        compiler_params=pltpu.CompilerParams(vmem_limit_bytes=32 * 2**20),
    )(lookup, before, after, near, up_weight, conv_weight)


def per_device(parents, parent_dest, skip, skip_dest, neighbours, up_weight, conv_weight):
    row, inner = lax.axis_index("gx"), lax.axis_index("gy")
    devices = LINES * COLUMNS
    place = jnp.stack([inner // COLUMNS, inner % COLUMNS, row * devices * BRICKS])
    first = first_pack(parent_dest, skip_dest, place, parents, skip)
    came = [first[0]]
    for j in range(1, COLUMNS):
        steps = [(i, i // COLUMNS * COLUMNS + column_at(i % COLUMNS, j)) for i in range(devices)]
        came.append(lax.ppermute(first[j], "gy", steps))
    messages = second_pack(place, came)
    arrived = [messages[0]]
    for k in range(1, LINES):
        steps = [(i, (i + HOPS[k] * COLUMNS) % devices) for i in range(devices)]
        arrived.append(lax.ppermute(messages[k], "gy", steps))
    own, surface, flag = unpack(arrived)
    own, surface, _ = lax.while_loop(
        lambda state: state[2][0] > 0,
        lambda state: (
            *dense_route(place, parents, parent_dest, skip, skip_dest),
            jnp.zeros_like(state[2]),
        ),
        (own, surface, flag),
    )
    whole = lax.axis_size(("gx", "gy"))
    up = [(i, i + 1) for i in range(whole - 1)]
    before = lax.ppermute(surface, ("gx", "gy"), up)
    after = lax.ppermute(surface, ("gx", "gy"), [(j, i) for i, j in up])
    me = row * devices + inner
    ahead = neighbours - me * BRICKS
    here = (neighbours >= 0) & (ahead >= 0) & (ahead < BRICKS)
    near_lookup = jnp.where(here, ahead, BRICKS)
    far = jnp.where(ahead < 0, ahead + BRICKS, ahead)
    far_lookup = jnp.where((neighbours >= 0) & ~here, far, 2 * BRICKS)
    up_weight = up_weight.reshape(4, 512, 128)
    conv_weight = conv_weight.reshape(3, 9 * 256, 128)
    near = convolve_near(
        near_lookup.reshape(-1), own, up_weight, conv_weight
    )
    return convolve_far(far_lookup.reshape(-1), before, after, near, up_weight, conv_weight)


def solution(mesh):
    placed = (
        P(("gx", "gy"), None, None),
        P(("gx", "gy")),
        P(("gx", "gy"), None, None),
        P(("gx", "gy")),
        P(("gx", "gy"), None),
        P(),
        P(),
    )
    return jax.shard_map(
        per_device,
        mesh=mesh,
        in_specs=placed,
        out_specs=P(("gx", "gy"), None, None),
        check_vma=False,
    )
```
